32 devices in a mesh: row: 4 (over y, x), col: 8 (over z, core).
Axes of the slice: x: 2, y: 2, z: 4, core: 2. Of those that a mesh axis runs over, the one named last changes fastest.
Arguments:
- amplitudes: bfloat16 [4096, 4096], P('row', 'col'), may hold values from -6 to 6
- df_factors: bfloat16 [4096, 1024], P('col', 'row'), may hold values from -0.25 to 0.25
- ladder: bfloat16 [64, 64], P(('row', 'col')), may hold values from -0.75 to 0.75
- occ_energy: float32 [200], replicated, may hold values from -2.5 to -0.3
- occ_index: int32 [8], replicated, may hold values from 0 to 199
- vir_energy: float32 [512], replicated, may hold values from 0.3 to 3
- vir_map: int32 [512], replicated, may hold values from 0 to 511, each once
Outputs:
- residual_update: bfloat16 [4096, 4096], P('row', 'col')
The draws below stay inside these ranges and needn't reach their ends.
All inputs are finite; a program needn't handle non-finite values.
Results may differ from the reference program's by a relative error of at most 0.0045.
The reference program's roundings to bfloat16 on the way (of `combined`, `fitted` and `hole_term`) count: a program that leaves them out, or rounds other values in their place, can miss the bound.
Values may be sent and summed in bfloat16 or wider, within the bound.
A program may use at most 64 MiB of HBM per device.

```python
import jax
import jax.numpy as jnp
from jax import lax

VIR = 512
AUX = 1024
NOCC = 200
OCC = 8
ORDER = 4096
PAIRS = 64


def with_ends(drawn, own_key, low, high):
    spot = [jax.random.randint(jax.random.fold_in(own_key, axis), (), 0, length) for axis, length in enumerate(drawn.shape)]
    longest = drawn.shape.index(max(drawn.shape))
    beside = spot[:longest] + [(spot[longest] + 1) % drawn.shape[longest]] + spot[longest + 1:]
    return drawn.at[tuple(spot)].set(low).at[tuple(beside)].set(high)


def with_spikes(drawn, rng, source, target, shards_of, factor):
    owner, partner = [(jnp.arange(drawn.shape[position]) // (drawn.shape[position] // shards_of)).reshape([-1 if axis == position else 1 for axis in range(drawn.ndim)]) for position in (source, target)]
    chosen = jax.random.permutation(rng, shards_of)[partner]
    strong = (owner == chosen) | (owner == (partner + shards_of // 2) % shards_of)
    return jnp.where(strong, factor * drawn, drawn)


def steps_of(own_key, extent, split, smallest, high):
    loudness = 1.0
    for position, parts in split:
        heights = jax.random.uniform(jax.random.fold_in(jax.random.fold_in(own_key, 6), position), (parts,), jnp.float32, smallest / len(split), high / len(split))
        loudness = loudness * jnp.repeat(jnp.exp(heights), extent[position] // parts).reshape((-1,) + (1,) * (len(extent) - 1 - position))
    return loudness


def gaussian(rng, dims, width, limit, shards=(), held_as=jnp.bfloat16):
    entries = width * jax.random.normal(rng, dims, jnp.float32)
    if shards:
        entries = entries * steps_of(rng, dims, shards, -0.22, 0.18)
    return jnp.clip(entries, -limit, limit).astype(held_as)


def heavy_noise(stream_key, extent, width, bound, shards, heavy, kind=jnp.bfloat16):
    drawn = width * jax.random.normal(stream_key, extent, jnp.float32)
    if shards:
        drawn = drawn * steps_of(stream_key, extent, shards, -0.22, 0.18)
    return jnp.clip(with_spikes(drawn, jax.random.fold_in(stream_key, 3), *heavy), -bound, bound).astype(kind)


def setup_inputs(seed: int = 0) -> dict:
    key_of = jax.random.split(jax.random.key(seed), 8)
    return {
        "amplitudes": gaussian(key_of[0], (ORDER, ORDER), 1.0, 6.0, ((0, 4), (1, 8))),
        "df_factors": heavy_noise(key_of[1], (ORDER, AUX), AUX ** -0.5, 0.25, ((0, 8), (1, 4)), (0, 1, 8, 2.0)),
        "ladder": gaussian(key_of[2], (PAIRS, PAIRS), PAIRS ** -0.5, 0.75, ((0, 32),)),
        "occ_energy": jnp.clip(jax.random.uniform(key_of[3], (NOCC,), jnp.float32, -2.5, -0.3), -2.5, -0.3),
        "occ_index": with_ends(jax.random.randint(key_of[4], (OCC,), 0, NOCC), jax.random.fold_in(key_of[4], 1), 0, NOCC - 1).astype(jnp.int32),
        "vir_energy": jnp.clip(jax.random.uniform(key_of[5], (VIR,), jnp.float32, 0.3, 3.0), 0.3, 3.0),
        "vir_map": jax.random.permutation(key_of[6], VIR).astype(jnp.int32),
    }


def reference(amplitudes, df_factors, ladder, occ_energy, occ_index, vir_energy, vir_map):
    order = OCC * VIR
    blocks = amplitudes.reshape(OCC, VIR, OCC, VIR)
    factors_wide = df_factors.astype(jnp.float32)

    def fit_rows(occ):
        slab = lax.dynamic_index_in_dim(blocks, occ, 0, keepdims=False)
        mirror = jnp.transpose(slab, (2, 1, 0))
        combined = (2.0 * slab.astype(jnp.float32) - mirror.astype(jnp.float32)).astype(jnp.bfloat16)
        return jnp.dot(combined.reshape(VIR, order).astype(jnp.float32), factors_wide)

    fitted = lax.map(fit_rows, jnp.arange(OCC, dtype=jnp.int32)).reshape(order, AUX).astype(jnp.bfloat16)
    pair_major = jnp.transpose(blocks, (0, 2, 1, 3)).reshape(OCC * OCC, VIR * VIR).astype(jnp.float32)
    ladder_rows = ladder.reshape(OCC, OCC, OCC * OCC).astype(jnp.float32)
    row_energy = occ_energy[occ_index]
    virtual = vir_energy[vir_map]

    def residual_rows(occ):
        fit_block = lax.dynamic_slice_in_dim(fitted, occ * VIR, VIR, 0).astype(jnp.float32)
        coulomb = jnp.dot(fit_block, factors_wide.T).reshape(VIR, OCC, VIR)
        weights = lax.dynamic_index_in_dim(ladder_rows, occ, 0, keepdims=False)
        hole_term = jnp.dot(weights, pair_major).astype(jnp.bfloat16)
        hole_term = lax.optimization_barrier(hole_term).astype(jnp.float32)
        hole_term = jnp.transpose(hole_term.reshape(OCC, VIR, VIR), (1, 0, 2))
        own_energy = lax.dynamic_index_in_dim(row_energy, occ, 0, keepdims=False)
        denominator = own_energy + row_energy[None, :, None] - virtual[:, None, None] - virtual[None, None, :]
        return ((coulomb + hole_term) / denominator).astype(jnp.bfloat16)

    result = lax.map(residual_rows, jnp.arange(OCC, dtype=jnp.int32))
    return result.reshape(order, order)
```

```python
import functools

import jax
import jax.numpy as jnp
from jax import lax
from jax.experimental import pallas as pl
from jax.experimental.pallas import tpu as pltpu
from jax.sharding import PartitionSpec as P

VIR = 512
MESH = pl.DeviceIdType.MESH
F32 = jnp.float32
BF16 = jnp.bfloat16


def lookup(values, positions):
    table = jnp.arange(values.shape[0], dtype=jnp.int32)
    matches = positions[:, None] == table[None, :]
    return jnp.sum(jnp.where(matches, values[None, :], 0.0), axis=1)


def by_collectives(amplitudes, df_factors, ladder, occ_energy, occ_index, vir_energy, vir_map):
    rows_tile, cols_tile = amplitudes.shape
    occ_row = rows_tile // VIR
    occ_col = cols_tile // VIR
    occ_all = occ_index.shape[0]
    vir_rows = VIR // lax.axis_size("row")
    vir_cols = VIR // lax.axis_size("col")
    blocks = amplitudes.reshape(occ_row, VIR, occ_col, VIR)
    mirror = jnp.transpose(blocks, (0, 3, 2, 1))
    combined = (2.0 * blocks.astype(F32) - mirror.astype(F32)).astype(BF16)
    combined = combined.reshape(rows_tile, cols_tile)
    factors = lax.all_gather(df_factors, "row", axis=1, tiled=True)
    partial_fit = jnp.dot(combined, factors, preferred_element_type=F32)
    contract = (((1,), (1,)), ((), ()))
    shared = lax.psum_scatter(partial_fit, "col", scatter_dimension=1, tiled=True).astype(BF16)
    fitted = lax.all_gather(shared, "col", axis=1, tiled=True)
    coulomb = lax.dot_general(fitted, factors, contract, preferred_element_type=F32)
    arranged = lax.all_to_all(
        lax.all_to_all(blocks, "row", split_axis=1, concat_axis=0, tiled=True),
        "col",
        split_axis=3,
        concat_axis=2,
        tiled=True,
    )
    pair_major = jnp.transpose(arranged, (0, 2, 1, 3)).reshape(
        occ_all * occ_all, vir_rows * vir_cols
    )
    hole_wide = jnp.dot(
        lax.all_gather(ladder, ("row", "col"), axis=0, tiled=True),
        pair_major,
        preferred_element_type=F32,
    )
    hole_term = hole_wide.astype(BF16)
    returned = jnp.transpose(hole_term.reshape(occ_all, occ_all, vir_rows, vir_cols), (0, 2, 1, 3))
    hole_tile = lax.all_to_all(
        lax.all_to_all(returned, "row", split_axis=0, concat_axis=1, tiled=True),
        "col",
        split_axis=2,
        concat_axis=3,
        tiled=True,
    )
    row_start = lax.axis_index("row") * occ_row
    col_start = lax.axis_index("col") * occ_col
    row_energy = lookup(occ_energy, lax.dynamic_slice_in_dim(occ_index, row_start, occ_row))
    col_energy = lookup(occ_energy, lax.dynamic_slice_in_dim(occ_index, col_start, occ_col))
    virtual = lookup(vir_energy, vir_map)
    denominator = (
        row_energy[:, None, None, None]
        + col_energy[None, None, :, None]
        - virtual[None, :, None, None]
        - virtual[None, None, None, :]
    )
    summed = coulomb.reshape(occ_row, VIR, occ_col, VIR) + hole_tile.astype(F32)
    return (summed / denominator).astype(BF16).reshape(rows_tile, cols_tile)


def kernel(
    R, C, amp, fac, lad, occ_e, occ_i, vir_e, vir_m, out,
    comb, factors, part, twin, rs_out, rs_in, fit, pairs, hole, hole_in, kron, lad_own, lad_all,
    vcol,
    fac_s, fac_r, fwd_s, fwd_r, lad_s, lad_r, tw_s, tw_r, rs_s, rs_r, ag_s, ag_r, rl_s, rl_r,
    back_s, back_r,
):
    nd = R * C
    Z = C // 2
    occ_row, _, sub, _ = amp.shape
    rows = occ_row * VIR
    chunk = rows // C
    q_cols = fac.shape[1]
    per_pair = lad.shape[0]
    n_pairs = lad.shape[1]
    r = lax.axis_index("row")
    c = lax.axis_index("col")
    me = r * C + c
    core = lax.rem(c, 2)
    z = lax.div(c, 2)
    other = 1 - core

    def place(d):
        return (lax.div(d, C), lax.rem(d, C))

    def peer(o):
        return lax.rem(me + o, nd)

    def send(src, dst, s, d, target):
        return pltpu.make_async_remote_copy(
            src_ref=src, dst_ref=dst, send_sem=s, recv_sem=d, device_id=target, device_id_type=MESH
        )

    barrier = pltpu.get_barrier_semaphore()

    @pl.loop(1, nd)
    def _(o):
        pl.semaphore_signal(barrier, inc=1, device_id=place(peer(o)), device_id_type=MESH)

    pl.semaphore_wait(barrier, nd - 1)

    def fac_copy(o):
        return send(
            fac, factors.at[r], fac_s.at[o], fac_r.at[r], (lax.rem(r + o, R), c)
        )

    for o in range(1, R):
        fac_copy(o).start()

    lad_own[...] = jnp.zeros_like(lad_own)
    lad_own[0:per_pair, 0:n_pairs] = lad[...].astype(F32)

    def fwd_copy(o):
        d = peer(o)
        return send(amp.at[:, d], pairs.at[r, :, c], fwd_s.at[o], fwd_r.at[me], place(d))

    def lad_copy(o):
        return send(lad_own, lad_all.at[me], lad_s.at[o], lad_r.at[me], place(peer(o)))

    @pl.loop(1, nd)
    def _(o):
        fwd_copy(o).start()
        lad_copy(o).start()

    for k in range(occ_row):
        slab = amp[k].reshape(VIR, VIR).astype(F32)
        comb[k * VIR:(k + 1) * VIR, :] = (2.0 * slab - slab.T).astype(BF16)
    factors[r] = fac[...]
    pairs[r, :, c] = amp[:, me]
    lad_all[me] = lad_own[...]

    def tw_copy(q):
        return send(part.at[q, :, other], twin.at[q], tw_s.at[q], tw_r.at[q], (r, 2 * z + other))

    def rs_copy(o, q):
        to = lax.rem(z + o, Z)
        return send(
            rs_out.at[q, to], rs_in.at[q, z], rs_s.at[o, q], rs_r.at[q, z], (r, 2 * to + core)
        )

    for o in range(R):
        q = lax.rem(r + o, R)
        if o:
            send(fac, factors.at[q], fac_s.at[o], fac_r.at[q], (r, c)).wait_recv()
        got = jnp.dot(comb[...], factors[q], preferred_element_type=F32)
        part[q] = got.reshape(Z, 2, chunk, q_cols)
        tw_copy(q).start()

    for o in range(R):
        q = lax.rem(r + o, R)
        tw_copy(q).wait_recv()
        rs_out[q] = (part[q, :, core] + twin[q]).astype(BF16)
        for step in range(1, Z):
            rs_copy(step, q).start()

    ids_r = lax.broadcasted_iota(jnp.int32, (VIR, VIR), 0)
    ids_c = lax.broadcasted_iota(jnp.int32, (VIR, VIR), 1)
    e_col = jnp.sum(jnp.where(ids_r == ids_c, vir_e[...], 0.0), axis=1, keepdims=True)
    v_row = jnp.sum(jnp.where(ids_r == vir_m[...], e_col, 0.0), axis=0, keepdims=True)
    vcol[...] = jnp.sum(jnp.where(ids_r == ids_c, v_row, 0.0), axis=1, keepdims=True)

    @pl.loop(1, nd)
    def _(o):
        d = peer(o)
        send(lad_own, lad_all.at[d], lad_s.at[o], lad_r.at[d], place(d)).wait_recv()

    shift = sub.bit_length() - 1
    wide = n_pairs * sub
    lad_flat = lad_all[...].reshape(nd * lad_own.shape[0], lad_own.shape[1]).astype(BF16)
    spread = (
        lax.broadcasted_iota(jnp.int32, (lad_own.shape[1], wide), 0)
        == (lax.broadcasted_iota(jnp.int32, (lad_own.shape[1], wide), 1) >> shift)
    )
    lad_wide = jnp.dot(
        lad_flat, spread.astype(F32).astype(BF16), preferred_element_type=F32
    ).astype(BF16)
    step_rows = 128

    @pl.loop(0, wide // step_rows)
    def _(n):
        at = pl.multiple_of(n * step_rows, step_rows)
        pair = (lax.broadcasted_iota(jnp.int32, (step_rows, lad_flat.shape[0]), 0) + at) >> shift
        held = lax.broadcasted_iota(jnp.int32, (step_rows, lad_flat.shape[0]), 1)
        pick = held == (lax.div(pair, per_pair) * lad_own.shape[0] + lax.rem(pair, per_pair))
        block = jnp.dot(pick.astype(F32).astype(BF16), lad_wide, preferred_element_type=F32)
        same = (lax.broadcasted_iota(jnp.int32, (step_rows, wide), 0) & (sub - 1)) == (
            lax.broadcasted_iota(jnp.int32, (step_rows, wide), 1) & (sub - 1)
        )
        kron[pl.ds(at, step_rows), :] = jnp.where(same, block, 0.0).astype(BF16)

    @pl.loop(1, nd)
    def _(o):
        d = peer(o)
        dr, dc = place(d)
        send(amp.at[:, d], pairs.at[dr, :, dc], fwd_s.at[o], fwd_r.at[d], (dr, dc)).wait_recv()

    row_blocks = wide // R
    for n in range(R):
        term = jnp.dot(
            kron[n * row_blocks:(n + 1) * row_blocks, :],
            pairs[...].reshape(wide, VIR),
            preferred_element_type=F32,
        )
        hole[n] = term.astype(BF16).reshape(occ_row, C, sub, VIR)

    def back_copy(o):
        d = peer(o)
        dr, dc = place(d)
        return send(hole.at[dr, :, dc], hole_in.at[:, me], back_s.at[o], back_r.at[me], (dr, dc))

    @pl.loop(1, nd)
    def _(o):
        back_copy(o).start()

    hole_in[:, me] = hole[r, :, c]

    for o in range(R):
        q = lax.rem(r + o, R)
        total = part[q, z, core] + twin[q, z]
        for step in range(1, Z):
            src = lax.rem(z + step, Z)
            send(
                rs_out.at[q, src], rs_in.at[q, src], rs_s.at[step, q], rs_r.at[q, src], (r, c)
            ).wait_recv()
            total = total + rs_in[q, src].astype(F32)
        fit[z, core, q] = total.astype(BF16)

    def ag_copy(o):
        to = lax.rem(z + o, Z)
        return send(
            fit.at[z, core], fit.at[z, core], ag_s.at[o], ag_r.at[z], (r, 2 * to + core)
        )

    def relay(src):
        return send(
            fit.at[src, core], fit.at[src, core], rl_s.at[src], rl_r.at[src], (r, 2 * z + other)
        )

    for o in range(1, Z):
        ag_copy(o).start()
    relay(z).start()

    @pl.loop(1, nd)
    def _(o):
        d = peer(o)
        send(hole.at[r, :, c], hole_in.at[:, d], back_s.at[o], back_r.at[d], place(d)).wait_recv()

    per_occ = VIR // chunk
    groups = chunk // sub
    energy_j = occ_e[occ_i[c]]

    def finish(src, which):
        n = 2 * src + which
        k = lax.div(n, per_occ)
        m = lax.rem(n, per_occ)
        acc = None
        for q in range(R):
            term = lax.dot_general(
                fit[src, which, q], factors[q], (((1,), (1,)), ((), ())),
                preferred_element_type=F32,
            )
            acc = term if acc is None else acc + term
        held = hole_in[k, pl.ds(m * groups, groups)].reshape(chunk, VIR).astype(F32)
        energy = occ_e[occ_i[r * occ_row + k]] + energy_j
        rows_at = pl.multiple_of(m * chunk, chunk)
        denominator = (energy - vcol[pl.ds(rows_at, chunk), :]) - v_row
        at = pl.multiple_of(n * chunk, chunk)
        out[pl.ds(at, chunk), :] = ((acc + held) / denominator).astype(BF16)

    finish(z, core)
    for o in range(1, Z):
        src = lax.rem(z + o, Z)
        send(fit.at[src, core], fit.at[src, core], ag_s.at[o], ag_r.at[src], (r, c)).wait_recv()
        relay(src).start()
        finish(src, core)
    for o in range(Z):
        src = lax.rem(z + o, Z)
        send(
            fit.at[src, other], fit.at[src, other], rl_s.at[src], rl_r.at[src], (r, c)
        ).wait_recv()
        finish(src, other)

    @pl.loop(1, nd)
    def _(o):
        fwd_copy(o).wait_send()
        lad_copy(o).wait_send()
        back_copy(o).wait_send()

    for o in range(1, R):
        fac_copy(o).wait_send()
    for q in range(R):
        tw_copy(q).wait_send()
        for o in range(1, Z):
            rs_copy(o, q).wait_send()
    for o in range(1, Z):
        ag_copy(o).wait_send()
    for o in range(Z):
        relay(o).wait_send()


def fused(R, C, amplitudes, df_factors, ladder, occ_energy, occ_index, vir_energy, vir_map):
    nd = R * C
    Z = C // 2
    rows, _ = amplitudes.shape
    occ_row = rows // VIR
    sub = VIR // nd
    chunk = rows // C
    depth, q_cols = df_factors.shape
    n_pairs = ladder.shape[1]
    wide = n_pairs * sub
    lad_rows = -(-ladder.shape[0] // 8) * 8
    lad_cols = -(-n_pairs // 128) * 128
    vmem = pl.BlockSpec(memory_space=pltpu.VMEM)
    smem = pl.BlockSpec(memory_space=pltpu.SMEM)
    dma = pltpu.SemaphoreType.DMA
    return pl.pallas_call(
        functools.partial(kernel, R, C),
        out_shape=jax.ShapeDtypeStruct((rows, VIR), BF16),
        in_specs=[vmem, vmem, vmem, smem, smem, vmem, vmem],
        out_specs=vmem,
        scratch_shapes=[
            pltpu.VMEM((rows, VIR), BF16),
            pltpu.VMEM((R, depth, q_cols), BF16),
            pltpu.VMEM((R, Z, 2, chunk, q_cols), F32),
            pltpu.VMEM((R, Z, chunk, q_cols), F32),
            pltpu.VMEM((R, Z, chunk, q_cols), BF16),
            pltpu.VMEM((R, Z, chunk, q_cols), BF16),
            pltpu.VMEM((Z, 2, R, chunk, q_cols), BF16),
            pltpu.VMEM((R, occ_row, C, sub, VIR), BF16),
            pltpu.VMEM((R, occ_row, C, sub, VIR), BF16),
            pltpu.VMEM((occ_row, nd, sub, VIR), BF16),
            pltpu.VMEM((wide, wide), BF16),
            pltpu.VMEM((lad_rows, lad_cols), F32),
            pltpu.VMEM((nd, lad_rows, lad_cols), F32),
            pltpu.VMEM((VIR, 1), F32),
            dma((R,)), dma((R,)),
            dma((nd,)), dma((nd,)),
            dma((nd,)), dma((nd,)),
            dma((R,)), dma((R,)),
            dma((Z, R)), dma((R, Z)),
            dma((Z,)), dma((Z,)),
            dma((Z,)), dma((Z,)),
            dma((nd,)), dma((nd,)),
        ],
        compiler_params=pltpu.CompilerParams(
            collective_id=0, has_side_effects=True, vmem_limit_bytes=48 * 2**20
        ),
    )(
        amplitudes.reshape(occ_row, nd, sub, VIR), df_factors, ladder, occ_energy, occ_index,
        vir_energy.reshape(1, VIR), vir_map.reshape(1, VIR),
    )


def shards(amplitudes, df_factors, *rest):
    R, C = lax.axis_size("row"), lax.axis_size("col")
    rows, cols = amplitudes.shape
    fits = (
        VIR % (16 * R * C) == 0
        and cols == VIR
        and C % 2 == 0
        and rows % (16 * C) == 0
        and VIR % (rows // C) == 0
        and (rows // C) % (VIR // (R * C)) == 0
        and df_factors.shape[1] % 128 == 0
    )
    if fits:
        return fused(R, C, amplitudes, df_factors, *rest)
    return by_collectives(amplitudes, df_factors, *rest)


def solution(mesh):
    placed = (P("row", "col"), P("col", "row"), P(("row", "col"), None), P(), P(), P(), P())
    return jax.shard_map(
        shards, mesh=mesh, in_specs=placed, out_specs=P("row", "col"), check_vma=False
    )
```

```python
import functools

import jax
import jax.numpy as jnp
from jax import lax
from jax.experimental import pallas as pl
from jax.experimental.pallas import tpu as pltpu
from jax.sharding import PartitionSpec as P

VIR = 512
MESH = pl.DeviceIdType.MESH
F32 = jnp.float32
BF16 = jnp.bfloat16


def lookup(values, positions):
    table = jnp.arange(values.shape[0], dtype=jnp.int32)
    matches = positions[:, None] == table[None, :]
    return jnp.sum(jnp.where(matches, values[None, :], 0.0), axis=1)


def by_collectives(amplitudes, df_factors, ladder, occ_energy, occ_index, vir_energy, vir_map):
    rows_tile, cols_tile = amplitudes.shape
    occ_row = rows_tile // VIR
    occ_col = cols_tile // VIR
    occ_all = occ_index.shape[0]
    vir_rows = VIR // lax.axis_size("row")
    vir_cols = VIR // lax.axis_size("col")
    blocks = amplitudes.reshape(occ_row, VIR, occ_col, VIR)
    mirror = jnp.transpose(blocks, (0, 3, 2, 1))
    combined = (2.0 * blocks.astype(F32) - mirror.astype(F32)).astype(BF16)
    combined = combined.reshape(rows_tile, cols_tile)
    factors = lax.all_gather(df_factors, "row", axis=1, tiled=True)
    partial_fit = jnp.dot(combined, factors, preferred_element_type=F32)
    contract = (((1,), (1,)), ((), ()))
    shared = lax.psum_scatter(partial_fit, "col", scatter_dimension=1, tiled=True).astype(BF16)
    fitted = lax.all_gather(shared, "col", axis=1, tiled=True)
    coulomb = lax.dot_general(fitted, factors, contract, preferred_element_type=F32)
    arranged = lax.all_to_all(
        lax.all_to_all(blocks, "row", split_axis=1, concat_axis=0, tiled=True),
        "col",
        split_axis=3,
        concat_axis=2,
        tiled=True,
    )
    pair_major = jnp.transpose(arranged, (0, 2, 1, 3)).reshape(
        occ_all * occ_all, vir_rows * vir_cols
    )
    hole_wide = jnp.dot(
        lax.all_gather(ladder, ("row", "col"), axis=0, tiled=True),
        pair_major,
        preferred_element_type=F32,
    )
    hole_term = hole_wide.astype(BF16)
    returned = jnp.transpose(hole_term.reshape(occ_all, occ_all, vir_rows, vir_cols), (0, 2, 1, 3))
    hole_tile = lax.all_to_all(
        lax.all_to_all(returned, "row", split_axis=0, concat_axis=1, tiled=True),
        "col",
        split_axis=2,
        concat_axis=3,
        tiled=True,
    )
    row_start = lax.axis_index("row") * occ_row
    col_start = lax.axis_index("col") * occ_col
    row_energy = lookup(occ_energy, lax.dynamic_slice_in_dim(occ_index, row_start, occ_row))
    col_energy = lookup(occ_energy, lax.dynamic_slice_in_dim(occ_index, col_start, occ_col))
    virtual = lookup(vir_energy, vir_map)
    denominator = (
        row_energy[:, None, None, None]
        + col_energy[None, None, :, None]
        - virtual[None, :, None, None]
        - virtual[None, None, None, :]
    )
    summed = coulomb.reshape(occ_row, VIR, occ_col, VIR) + hole_tile.astype(F32)
    return (summed / denominator).astype(BF16).reshape(rows_tile, cols_tile)


def kernel(
    R, C, amp, fac, lad, occ_e, occ_i, vir_e, vir_m, out,
    amp_v, lad_v, e_v, m_v, occ_ev, occ_iv, out_v,
    comb, factors, part, twin, out1, in1, out2, in2, fit, pairs, hole, hole_in, kron, lad_own,
    lad_all, vcol,
    loc, put, fac_s, fac_r, fwd_s, fwd_r, lad_s, lad_r, tw_s, tw_r, s1_s, s1_r, s2_s, s2_r,
    g1_s, g1_r, g2_s, g2_r, rl_s, rl_r, back_s, back_r,
):
    nd = R * C
    Z = C // 2
    occ_row, _, sub, _ = amp.shape
    rows = occ_row * VIR
    chunk = rows // C
    q_cols = fac.shape[1]
    per_pair = lad.shape[0]
    n_pairs = lad.shape[1]
    r = lax.axis_index("row")
    c = lax.axis_index("col")
    me = r * C + c
    core = lax.rem(c, 2)
    z = lax.div(c, 2)
    other = 1 - core
    near = z + 1 - 2 * lax.rem(z, 2)
    far = lax.rem(z + 2, Z)
    far_near = lax.rem(near + 2, Z)

    def place(d):
        return (lax.div(d, C), lax.rem(d, C))

    def peer(o):
        return lax.rem(me + o, nd)

    def send(src, dst, s, d, target):
        return pltpu.make_async_remote_copy(
            src_ref=src, dst_ref=dst, send_sem=s, recv_sem=d, device_id=target, device_id_type=MESH
        )

    own_copies = [
        pltpu.make_async_copy(src, dst, loc.at[n])
        for n, (src, dst) in enumerate((
            (lad, lad_v), (amp, amp_v), (fac, factors.at[r]), (amp.at[:, me], pairs.at[r, :, c]),
            (vir_e, e_v), (vir_m, m_v), (occ_e, occ_ev), (occ_i, occ_iv),
        ))
    ]
    for copy in own_copies:
        copy.start()

    barrier = pltpu.get_barrier_semaphore()

    @pl.loop(1, nd)
    def _(o):
        pl.semaphore_signal(barrier, inc=1, device_id=place(peer(o)), device_id_type=MESH)

    lad_own[...] = jnp.zeros_like(lad_own)
    own_copies[0].wait()
    lad_own[0:per_pair, 0:n_pairs] = lad_v[...].astype(F32)
    lad_all[me] = lad_own[...]

    pl.semaphore_wait(barrier, nd - 1)

    def fac_copy(o):
        return send(
            fac, factors.at[r], fac_s.at[o], fac_r.at[r], (lax.rem(r + o, R), c)
        )

    for o in range(1, R):
        fac_copy(o).start()

    def fwd_copy(o):
        d = peer(o)
        return send(amp.at[:, d], pairs.at[r, :, c], fwd_s.at[o], fwd_r.at[me], place(d))

    def lad_copy(o):
        return send(lad_own, lad_all.at[me], lad_s.at[o], lad_r.at[me], place(peer(o)))

    @pl.loop(1, nd)
    def _(o):
        fwd_copy(o).start()
        lad_copy(o).start()

    own_copies[1].wait()
    for k in range(occ_row):
        slab = amp_v[k].reshape(VIR, VIR).astype(F32)
        comb[k * VIR:(k + 1) * VIR, :] = (2.0 * slab - slab.T).astype(BF16)
    own_copies[2].wait()

    def tw_copy(q):
        return send(part.at[q, :, other], twin.at[q], tw_s.at[q], tw_r.at[q], (r, 2 * z + other))

    def s1_copy(q):
        return send(out1.at[q], in1.at[q], s1_s.at[q], s1_r.at[q], (r, 2 * near + core))

    def s2_copy(q):
        return send(out2.at[q], in2.at[q], s2_s.at[q], s2_r.at[q], (r, 2 * far + core))

    def g1_copy(q):
        return send(
            fit.at[z, core, q], fit.at[z, core, q], g1_s.at[q], g1_r.at[q], (r, 2 * far + core)
        )

    def g2_copy(which, q):
        src = far if which else z
        return send(
            fit.at[src, core, q], fit.at[src, core, q], g2_s.at[which, q], g2_r.at[which, q],
            (r, 2 * near + core),
        )

    def relay(src):
        return send(
            fit.at[src, core], fit.at[src, core], rl_s.at[src], rl_r.at[src], (r, 2 * z + other)
        )

    order = [lax.rem(r + o, R) for o in range(R)]

    for o, q in enumerate(order):
        if o:
            send(fac, factors.at[q], fac_s.at[o], fac_r.at[q], (r, c)).wait_recv()
        got = jnp.dot(comb[...], factors[q], preferred_element_type=F32)
        part[q] = got.reshape(Z, 2, chunk, q_cols)
        tw_copy(q).start()

    for q in order:
        tw_copy(q).wait_recv()
        out1[q, 0] = (part[q, near, core] + twin[q, near]).astype(BF16)
        out1[q, 1] = (part[q, far_near, core] + twin[q, far_near]).astype(BF16)
        s1_copy(q).start()

    for copy in own_copies[4:]:
        copy.wait()
    ids_r = lax.broadcasted_iota(jnp.int32, (VIR, VIR), 0)
    ids_c = lax.broadcasted_iota(jnp.int32, (VIR, VIR), 1)
    e_col = jnp.sum(jnp.where(ids_r == ids_c, e_v[...], 0.0), axis=1, keepdims=True)
    v_row = jnp.sum(jnp.where(ids_r == m_v[...], e_col, 0.0), axis=0, keepdims=True)
    vcol[...] = jnp.sum(jnp.where(ids_r == ids_c, v_row, 0.0), axis=1, keepdims=True)

    @pl.loop(1, nd)
    def _(o):
        d = peer(o)
        send(lad_own, lad_all.at[d], lad_s.at[o], lad_r.at[d], place(d)).wait_recv()

    shift = sub.bit_length() - 1
    wide = n_pairs * sub
    lad_flat = lad_all[...].reshape(nd * lad_own.shape[0], lad_own.shape[1]).astype(BF16)
    spread = (
        lax.broadcasted_iota(jnp.int32, (lad_own.shape[1], wide), 0)
        == (lax.broadcasted_iota(jnp.int32, (lad_own.shape[1], wide), 1) >> shift)
    )
    lad_wide = jnp.dot(
        lad_flat, spread.astype(F32).astype(BF16), preferred_element_type=F32
    ).astype(BF16)
    step_rows = 128

    @pl.loop(0, wide // step_rows)
    def _(n):
        at = pl.multiple_of(n * step_rows, step_rows)
        pair = (lax.broadcasted_iota(jnp.int32, (step_rows, lad_flat.shape[0]), 0) + at) >> shift
        held = lax.broadcasted_iota(jnp.int32, (step_rows, lad_flat.shape[0]), 1)
        pick = held == (lax.div(pair, per_pair) * lad_own.shape[0] + lax.rem(pair, per_pair))
        block = jnp.dot(pick.astype(F32).astype(BF16), lad_wide, preferred_element_type=F32)
        same = (lax.broadcasted_iota(jnp.int32, (step_rows, wide), 0) & (sub - 1)) == (
            lax.broadcasted_iota(jnp.int32, (step_rows, wide), 1) & (sub - 1)
        )
        kron[pl.ds(at, step_rows), :] = jnp.where(same, block, 0.0).astype(BF16)

    own_copies[3].wait()

    @pl.loop(1, nd)
    def _(o):
        d = peer(o)
        dr, dc = place(d)
        send(amp.at[:, d], pairs.at[dr, :, dc], fwd_s.at[o], fwd_r.at[d], (dr, dc)).wait_recv()

    row_blocks = wide // R
    for n in range(R):
        term = jnp.dot(
            kron[n * row_blocks:(n + 1) * row_blocks, :],
            pairs[...].reshape(wide, VIR),
            preferred_element_type=F32,
        )
        hole[n] = term.astype(BF16).reshape(occ_row, C, sub, VIR)

    def back_copy(o):
        d = peer(o)
        dr, dc = place(d)
        return send(hole.at[dr, :, dc], hole_in.at[:, me], back_s.at[o], back_r.at[me], (dr, dc))

    @pl.loop(1, nd // 2)
    def _(o):
        back_copy(o).start()

    for q in order:
        s1_copy(q).wait_recv()
        out2[q] = ((part[q, far, core] + twin[q, far]) + in1[q, 1].astype(F32)).astype(BF16)
        s2_copy(q).start()

    @pl.loop(nd // 2, nd)
    def _(o):
        back_copy(o).start()

    hole_in[:, me] = hole[r, :, c]

    for q in order:
        s2_copy(q).wait_recv()
        total = (part[q, z, core] + twin[q, z]) + in1[q, 0].astype(F32)
        fit[z, core, q] = (total + in2[q].astype(F32)).astype(BF16)
        g1_copy(q).start()
        g2_copy(0, q).start()
    relay(z).start()

    def g1_wait(q):
        send(
            fit.at[far, core, q], fit.at[far, core, q], g1_s.at[q], g1_r.at[q], (r, c)
        ).wait_recv()

    def g2_wait(which, q):
        src = far_near if which else near
        send(
            fit.at[src, core, q], fit.at[src, core, q], g2_s.at[which, q], g2_r.at[which, q],
            (r, c),
        ).wait_recv()

    for q in order:
        g1_wait(q)
        g2_copy(1, q).start()
    relay(far).start()

    @pl.loop(1, nd)
    def _(o):
        d = peer(o)
        send(hole.at[r, :, c], hole_in.at[:, d], back_s.at[o], back_r.at[d], place(d)).wait_recv()

    per_occ = VIR // chunk
    groups = chunk // sub
    energy_j = occ_ev[occ_iv[c]]

    def out_copy(n):
        at = pl.ds(pl.multiple_of(n * chunk, chunk), chunk)
        return pltpu.make_async_copy(out_v.at[at, :], out.at[at, :], put.at[n])

    def finish(src, which):
        n = 2 * src + which
        k = lax.div(n, per_occ)
        m = lax.rem(n, per_occ)
        acc = None
        for q in range(R):
            term = lax.dot_general(
                fit[src, which, q], factors[q], (((1,), (1,)), ((), ())),
                preferred_element_type=F32,
            )
            acc = term if acc is None else acc + term
        held = hole_in[k, pl.ds(m * groups, groups)].reshape(chunk, VIR).astype(F32)
        energy = occ_ev[occ_iv[r * occ_row + k]] + energy_j
        rows_at = pl.multiple_of(m * chunk, chunk)
        denominator = (energy - vcol[pl.ds(rows_at, chunk), :]) - v_row
        at = pl.multiple_of(n * chunk, chunk)
        out_v[pl.ds(at, chunk), :] = ((acc + held) / denominator).astype(BF16)
        out_copy(n).start()

    def relay_wait(src):
        send(
            fit.at[src, other], fit.at[src, other], rl_s.at[src], rl_r.at[src], (r, c)
        ).wait_recv()

    finish(z, core)
    finish(far, core)
    relay_wait(z)
    finish(z, other)
    for which, src in ((0, near), (1, far_near)):
        for q in order:
            g2_wait(which, q)
        relay(src).start()
        finish(src, core)
        if which == 0:
            relay_wait(far)
            finish(far, other)
    for src in (near, far_near):
        relay_wait(src)
        finish(src, other)

    @pl.loop(1, nd)
    def _(o):
        fwd_copy(o).wait_send()
        lad_copy(o).wait_send()
        back_copy(o).wait_send()

    for o in range(1, R):
        fac_copy(o).wait_send()
    for q in range(R):
        tw_copy(q).wait_send()
        s1_copy(q).wait_send()
        s2_copy(q).wait_send()
        g1_copy(q).wait_send()
        g2_copy(0, q).wait_send()
        g2_copy(1, q).wait_send()
    for o in range(Z):
        relay(o).wait_send()
    for n in range(C):
        out_copy(n).wait()


def fused(R, C, amplitudes, df_factors, ladder, occ_energy, occ_index, vir_energy, vir_map):
    nd = R * C
    Z = C // 2
    rows, _ = amplitudes.shape
    occ_row = rows // VIR
    sub = VIR // nd
    chunk = rows // C
    depth, q_cols = df_factors.shape
    n_pairs = ladder.shape[1]
    wide = n_pairs * sub
    lad_rows = -(-ladder.shape[0] // 8) * 8
    lad_cols = -(-n_pairs // 128) * 128
    hbm = pl.BlockSpec(memory_space=pl.ANY)
    dma = pltpu.SemaphoreType.DMA
    return pl.pallas_call(
        functools.partial(kernel, R, C),
        out_shape=jax.ShapeDtypeStruct((rows, VIR), BF16),
        in_specs=[hbm] * 7,
        out_specs=hbm,
        scratch_shapes=[
            pltpu.VMEM((occ_row, nd, sub, VIR), BF16),
            pltpu.VMEM(ladder.shape, BF16),
            pltpu.VMEM((1, VIR), F32),
            pltpu.VMEM((1, VIR), jnp.int32),
            pltpu.SMEM(occ_energy.shape, F32),
            pltpu.SMEM(occ_index.shape, jnp.int32),
            pltpu.VMEM((rows, VIR), BF16),
            pltpu.VMEM((rows, VIR), BF16),
            pltpu.VMEM((R, depth, q_cols), BF16),
            pltpu.VMEM((R, Z, 2, chunk, q_cols), F32),
            pltpu.VMEM((R, Z, chunk, q_cols), F32),
            pltpu.VMEM((R, 2, chunk, q_cols), BF16),
            pltpu.VMEM((R, 2, chunk, q_cols), BF16),
            pltpu.VMEM((R, chunk, q_cols), BF16),
            pltpu.VMEM((R, chunk, q_cols), BF16),
            pltpu.VMEM((Z, 2, R, chunk, q_cols), BF16),
            pltpu.VMEM((R, occ_row, C, sub, VIR), BF16),
            pltpu.VMEM((R, occ_row, C, sub, VIR), BF16),
            pltpu.VMEM((occ_row, nd, sub, VIR), BF16),
            pltpu.VMEM((wide, wide), BF16),
            pltpu.VMEM((lad_rows, lad_cols), F32),
            pltpu.VMEM((nd, lad_rows, lad_cols), F32),
            pltpu.VMEM((VIR, 1), F32),
            dma((8,)), dma((C,)),
            dma((R,)), dma((R,)),
            dma((nd,)), dma((nd,)),
            dma((nd,)), dma((nd,)),
            dma((R,)), dma((R,)),
            dma((R,)), dma((R,)),
            dma((R,)), dma((R,)),
            dma((R,)), dma((R,)),
            dma((2, R)), dma((2, R)),
            dma((Z,)), dma((Z,)),
            dma((nd,)), dma((nd,)),
        ],
        compiler_params=pltpu.CompilerParams(
            collective_id=0, has_side_effects=True, vmem_limit_bytes=56 * 2**20
        ),
    )(
        amplitudes.reshape(occ_row, nd, sub, VIR), df_factors, ladder, occ_energy, occ_index,
        vir_energy.reshape(1, VIR), vir_map.reshape(1, VIR),
    )


def shards(amplitudes, df_factors, *rest):
    R, C = lax.axis_size("row"), lax.axis_size("col")
    rows, cols = amplitudes.shape
    fits = (
        VIR % (16 * R * C) == 0
        and cols == VIR
        and C == 8
        and rows % (16 * C) == 0
        and VIR % (rows // C) == 0
        and (rows // C) % (VIR // (R * C)) == 0
        and df_factors.shape[1] % 128 == 0
    )
    if fits:
        return fused(R, C, amplitudes, df_factors, *rest)
    return by_collectives(amplitudes, df_factors, *rest)


def solution(mesh):
    placed = (P("row", "col"), P("col", "row"), P(("row", "col"), None), P(), P(), P(), P())
    return jax.shard_map(
        shards, mesh=mesh, in_specs=placed, out_specs=P("row", "col"), check_vma=False
    )
```

```python
import functools

import jax
import jax.numpy as jnp
from jax import lax
from jax.experimental import pallas as pl
from jax.experimental.pallas import tpu as pltpu
from jax.sharding import PartitionSpec as P

VIR = 512
MESH = pl.DeviceIdType.MESH
F32 = jnp.float32
BF16 = jnp.bfloat16


def lookup(values, positions):
    table = jnp.arange(values.shape[0], dtype=jnp.int32)
    matches = positions[:, None] == table[None, :]
    return jnp.sum(jnp.where(matches, values[None, :], 0.0), axis=1)


def by_collectives(amplitudes, df_factors, ladder, occ_energy, occ_index, vir_energy, vir_map):
    rows_tile, cols_tile = amplitudes.shape
    occ_row = rows_tile // VIR
    occ_col = cols_tile // VIR
    occ_all = occ_index.shape[0]
    vir_rows = VIR // lax.axis_size("row")
    vir_cols = VIR // lax.axis_size("col")
    blocks = amplitudes.reshape(occ_row, VIR, occ_col, VIR)
    mirror = jnp.transpose(blocks, (0, 3, 2, 1))
    combined = (2.0 * blocks.astype(F32) - mirror.astype(F32)).astype(BF16)
    combined = combined.reshape(rows_tile, cols_tile)
    factors = lax.all_gather(df_factors, "row", axis=1, tiled=True)
    partial_fit = jnp.dot(combined, factors, preferred_element_type=F32)
    contract = (((1,), (1,)), ((), ()))
    shared = lax.psum_scatter(partial_fit, "col", scatter_dimension=1, tiled=True).astype(BF16)
    fitted = lax.all_gather(shared, "col", axis=1, tiled=True)
    coulomb = lax.dot_general(fitted, factors, contract, preferred_element_type=F32)
    arranged = lax.all_to_all(
        lax.all_to_all(blocks, "row", split_axis=1, concat_axis=0, tiled=True),
        "col",
        split_axis=3,
        concat_axis=2,
        tiled=True,
    )
    pair_major = jnp.transpose(arranged, (0, 2, 1, 3)).reshape(
        occ_all * occ_all, vir_rows * vir_cols
    )
    hole_wide = jnp.dot(
        lax.all_gather(ladder, ("row", "col"), axis=0, tiled=True),
        pair_major,
        preferred_element_type=F32,
    )
    hole_term = hole_wide.astype(BF16)
    returned = jnp.transpose(hole_term.reshape(occ_all, occ_all, vir_rows, vir_cols), (0, 2, 1, 3))
    hole_tile = lax.all_to_all(
        lax.all_to_all(returned, "row", split_axis=0, concat_axis=1, tiled=True),
        "col",
        split_axis=2,
        concat_axis=3,
        tiled=True,
    )
    row_start = lax.axis_index("row") * occ_row
    col_start = lax.axis_index("col") * occ_col
    row_energy = lookup(occ_energy, lax.dynamic_slice_in_dim(occ_index, row_start, occ_row))
    col_energy = lookup(occ_energy, lax.dynamic_slice_in_dim(occ_index, col_start, occ_col))
    virtual = lookup(vir_energy, vir_map)
    denominator = (
        row_energy[:, None, None, None]
        + col_energy[None, None, :, None]
        - virtual[None, :, None, None]
        - virtual[None, None, None, :]
    )
    summed = coulomb.reshape(occ_row, VIR, occ_col, VIR) + hole_tile.astype(F32)
    return (summed / denominator).astype(BF16).reshape(rows_tile, cols_tile)


def kernel(
    R, C, amp, fac, lad, occ_e, occ_i, vir_e, vir_m, out,
    amp_v, lad_v, e_v, m_v, occ_ev, occ_iv,
    comb, factors, part, twin, out1, in1, out2, in2, fit, pairs, hole, hole_in, kron, lad_own,
    lad_all, inverse, coul,
    loc, fac_s, fac_r, fwd_s, fwd_r, lad_s, lad_r, tw_s, tw_r, s1_s, s1_r, s2_s, s2_r,
    g1_s, g1_r, g2_s, g2_r, rl_s, rl_r, back_s, back_r,
):
    nd = R * C
    Z = C // 2
    occ_row, _, sub, _ = amp.shape
    rows = occ_row * VIR
    chunk = rows // C
    q_cols = fac.shape[1]
    per_pair = lad.shape[0]
    n_pairs = lad.shape[1]
    r = lax.axis_index("row")
    c = lax.axis_index("col")
    me = r * C + c
    core = lax.rem(c, 2)
    z = lax.div(c, 2)
    other = 1 - core
    near = z + 1 - 2 * lax.rem(z, 2)
    far = lax.rem(z + 2, Z)
    far_near = lax.rem(near + 2, Z)

    def place(d):
        return (lax.div(d, C), lax.rem(d, C))

    def peer(o):
        return lax.rem(me + o, nd)

    def send(src, dst, s, d, target):
        return pltpu.make_async_remote_copy(
            src_ref=src, dst_ref=dst, send_sem=s, recv_sem=d, device_id=target, device_id_type=MESH
        )

    own_copies = [
        pltpu.make_async_copy(src, dst, loc.at[n])
        for n, (src, dst) in enumerate((
            (lad, lad_v), (amp, amp_v), (fac, factors.at[r]), (amp.at[:, me], pairs.at[r, :, c]),
            (vir_e, e_v), (vir_m, m_v), (occ_e, occ_ev), (occ_i, occ_iv),
        ))
    ]
    for copy in own_copies:
        copy.start()

    barrier = pltpu.get_barrier_semaphore()

    @pl.loop(1, nd)
    def _(o):
        pl.semaphore_signal(barrier, inc=1, device_id=place(peer(o)), device_id_type=MESH)

    lad_own[...] = jnp.zeros_like(lad_own)
    own_copies[0].wait()
    lad_own[0:per_pair, 0:n_pairs] = lad_v[...].astype(F32)
    lad_all[me] = lad_own[...]

    pl.semaphore_wait(barrier, nd - 1)

    def fac_copy(o):
        return send(
            fac, factors.at[r], fac_s.at[o], fac_r.at[r], (lax.rem(r + o, R), c)
        )

    for o in range(1, R):
        fac_copy(o).start()

    def fwd_copy(o):
        d = peer(o)
        return send(amp.at[:, d], pairs.at[r, :, c], fwd_s.at[o], fwd_r.at[me], place(d))

    def lad_copy(o):
        return send(lad_own, lad_all.at[me], lad_s.at[o], lad_r.at[me], place(peer(o)))

    def fwd_start(lo, hi):
        @pl.loop(lo, hi)
        def _(o):
            fwd_copy(o).start()

    first = nd // 2
    batch = -(-(nd - first) // R)

    @pl.loop(1, nd)
    def _(o):
        lad_copy(o).start()

    fwd_start(1, first)

    own_copies[1].wait()
    for k in range(occ_row):
        slab = amp_v[k].reshape(VIR, VIR).astype(F32)
        comb[k * VIR:(k + 1) * VIR, :] = (2.0 * slab - slab.T).astype(BF16)
    own_copies[2].wait()

    def tw_copy(q):
        return send(part.at[q, :, other], twin.at[q], tw_s.at[q], tw_r.at[q], (r, 2 * z + other))

    def s1_copy(q):
        return send(out1.at[q], in1.at[q], s1_s.at[q], s1_r.at[q], (r, 2 * near + core))

    def s2_copy(q):
        return send(out2.at[q], in2.at[q], s2_s.at[q], s2_r.at[q], (r, 2 * far + core))

    def g1_copy(q):
        return send(
            fit.at[z, core, q], fit.at[z, core, q], g1_s.at[q], g1_r.at[q], (r, 2 * far + core)
        )

    def g2_copy(which, q):
        src = far if which else z
        return send(
            fit.at[src, core, q], fit.at[src, core, q], g2_s.at[which, q], g2_r.at[which, q],
            (r, 2 * near + core),
        )

    def relay(src):
        return send(
            fit.at[src, core], fit.at[src, core], rl_s.at[src], rl_r.at[src], (r, 2 * z + other)
        )

    order = [lax.rem(r + o, R) for o in range(R)]

    for o, q in enumerate(order):
        if o:
            send(fac, factors.at[q], fac_s.at[o], fac_r.at[q], (r, c)).wait_recv()
        got = jnp.dot(comb[...], factors[q], preferred_element_type=F32)
        part[q] = got.reshape(Z, 2, chunk, q_cols)
        tw_copy(q).start()

    for o, q in enumerate(order):
        tw_copy(q).wait_recv()
        out1[q, 0] = (part[q, near, core] + twin[q, near]).astype(BF16)
        out1[q, 1] = (part[q, far_near, core] + twin[q, far_near]).astype(BF16)
        s1_copy(q).start()
        fwd_start(first + o * batch, min(first + (o + 1) * batch, nd))

    for copy in own_copies[4:]:
        copy.wait()
    ids_r = lax.broadcasted_iota(jnp.int32, (VIR, VIR), 0)
    ids_c = lax.broadcasted_iota(jnp.int32, (VIR, VIR), 1)
    e_col = jnp.sum(jnp.where(ids_r == ids_c, e_v[...], 0.0), axis=1, keepdims=True)
    v_row = jnp.sum(jnp.where(ids_r == m_v[...], e_col, 0.0), axis=0, keepdims=True)
    v_col = jnp.sum(jnp.where(ids_r == ids_c, v_row, 0.0), axis=1, keepdims=True)
    energy_j = occ_ev[occ_iv[c]]
    for k in range(occ_row):
        energy = occ_ev[occ_iv[r * occ_row + k]] + energy_j
        inverse[k * VIR:(k + 1) * VIR, :] = 1.0 / ((energy - v_col) - v_row)

    @pl.loop(1, nd)
    def _(o):
        d = peer(o)
        send(lad_own, lad_all.at[d], lad_s.at[o], lad_r.at[d], place(d)).wait_recv()

    shift = sub.bit_length() - 1
    wide = n_pairs * sub
    lad_flat = lad_all[...].reshape(nd * lad_own.shape[0], lad_own.shape[1]).astype(BF16)
    spread = (
        lax.broadcasted_iota(jnp.int32, (lad_own.shape[1], wide), 0)
        == (lax.broadcasted_iota(jnp.int32, (lad_own.shape[1], wide), 1) >> shift)
    )
    lad_wide = jnp.dot(
        lad_flat, spread.astype(F32).astype(BF16), preferred_element_type=F32
    ).astype(BF16)
    step_rows = 128

    @pl.loop(0, wide // step_rows)
    def _(n):
        at = pl.multiple_of(n * step_rows, step_rows)
        pair = (lax.broadcasted_iota(jnp.int32, (step_rows, lad_flat.shape[0]), 0) + at) >> shift
        held = lax.broadcasted_iota(jnp.int32, (step_rows, lad_flat.shape[0]), 1)
        pick = held == (lax.div(pair, per_pair) * lad_own.shape[0] + lax.rem(pair, per_pair))
        block = jnp.dot(pick.astype(F32).astype(BF16), lad_wide, preferred_element_type=F32)
        same = (lax.broadcasted_iota(jnp.int32, (step_rows, wide), 0) & (sub - 1)) == (
            lax.broadcasted_iota(jnp.int32, (step_rows, wide), 1) & (sub - 1)
        )
        kron[pl.ds(at, step_rows), :] = jnp.where(same, block, 0.0).astype(BF16)

    own_copies[3].wait()

    @pl.loop(1, nd)
    def _(o):
        d = peer(o)
        dr, dc = place(d)
        send(amp.at[:, d], pairs.at[dr, :, dc], fwd_s.at[o], fwd_r.at[d], (dr, dc)).wait_recv()

    row_blocks = wide // R
    for n in range(R):
        term = jnp.dot(
            kron[n * row_blocks:(n + 1) * row_blocks, :],
            pairs[...].reshape(wide, VIR),
            preferred_element_type=F32,
        )
        hole[n] = term.astype(BF16).reshape(occ_row, C, sub, VIR)

    def back_copy(o):
        d = peer(o)
        dr, dc = place(d)
        return send(hole.at[dr, :, dc], hole_in.at[:, me], back_s.at[o], back_r.at[me], (dr, dc))

    def back_start(lo, hi):
        @pl.loop(lo, hi)
        def _(o):
            back_copy(o).start()

    first = nd // 4
    batch = -(-(nd - first) // (2 * R))

    def back_batch(n):
        back_start(first + n * batch, min(first + (n + 1) * batch, nd))

    back_start(1, first)

    for o, q in enumerate(order):
        s1_copy(q).wait_recv()
        out2[q] = ((part[q, far, core] + twin[q, far]) + in1[q, 1].astype(F32)).astype(BF16)
        s2_copy(q).start()
        back_batch(o)

    hole_in[:, me] = hole[r, :, c]

    for o, q in enumerate(order):
        s2_copy(q).wait_recv()
        total = (part[q, z, core] + twin[q, z]) + in1[q, 0].astype(F32)
        fit[z, core, q] = (total + in2[q].astype(F32)).astype(BF16)
        g1_copy(q).start()
        g2_copy(0, q).start()
        back_batch(R + o)
    relay(z).start()

    def g1_wait(q):
        send(
            fit.at[far, core, q], fit.at[far, core, q], g1_s.at[q], g1_r.at[q], (r, c)
        ).wait_recv()

    def g2_wait(which, q):
        src = far_near if which else near
        send(
            fit.at[src, core, q], fit.at[src, core, q], g2_s.at[which, q], g2_r.at[which, q],
            (r, c),
        ).wait_recv()

    per_occ = VIR // chunk
    groups = chunk // sub

    def rows_of(n):
        return pl.ds(pl.multiple_of(n * chunk, chunk), chunk)

    def fitted_dot(src, which):
        acc = None
        for q in range(R):
            term = lax.dot_general(
                fit[src, which, q], factors[q], (((1,), (1,)), ((), ())),
                preferred_element_type=F32,
            )
            acc = term if acc is None else acc + term
        return acc

    def finish(src, which, acc):
        n = 2 * src + which
        k = lax.div(n, per_occ)
        m = lax.rem(n, per_occ)
        held = hole_in[k, pl.ds(m * groups, groups)].reshape(chunk, VIR).astype(F32)
        out[rows_of(n), :] = ((acc + held) * inverse[rows_of(n), :]).astype(BF16)

    def relay_wait(src):
        send(
            fit.at[src, other], fit.at[src, other], rl_s.at[src], rl_r.at[src], (r, c)
        ).wait_recv()

    coul[0] = fitted_dot(z, core)
    for q in order:
        g1_wait(q)
        g2_copy(1, q).start()
    relay(far).start()
    coul[1] = fitted_dot(far, core)
    relay_wait(z)
    coul[2] = fitted_dot(z, other)
    relay_wait(far)
    coul[3] = fitted_dot(far, other)

    @pl.loop(1, nd)
    def _(o):
        d = peer(o)
        send(hole.at[r, :, c], hole_in.at[:, d], back_s.at[o], back_r.at[d], place(d)).wait_recv()

    finish(z, core, coul[0])
    finish(far, core, coul[1])
    finish(z, other, coul[2])
    finish(far, other, coul[3])
    for which, src in ((0, near), (1, far_near)):
        for q in order:
            g2_wait(which, q)
        relay(src).start()
        finish(src, core, fitted_dot(src, core))
    for src in (near, far_near):
        relay_wait(src)
        finish(src, other, fitted_dot(src, other))

    @pl.loop(1, nd)
    def _(o):
        fwd_copy(o).wait_send()
        lad_copy(o).wait_send()
        back_copy(o).wait_send()

    for o in range(1, R):
        fac_copy(o).wait_send()
    for q in range(R):
        tw_copy(q).wait_send()
        s1_copy(q).wait_send()
        s2_copy(q).wait_send()
        g1_copy(q).wait_send()
        g2_copy(0, q).wait_send()
        g2_copy(1, q).wait_send()
    for o in range(Z):
        relay(o).wait_send()


def fused(R, C, amplitudes, df_factors, ladder, occ_energy, occ_index, vir_energy, vir_map):
    nd = R * C
    Z = C // 2
    rows, _ = amplitudes.shape
    occ_row = rows // VIR
    sub = VIR // nd
    chunk = rows // C
    depth, q_cols = df_factors.shape
    n_pairs = ladder.shape[1]
    wide = n_pairs * sub
    lad_rows = -(-ladder.shape[0] // 8) * 8
    lad_cols = -(-n_pairs // 128) * 128
    hbm = pl.BlockSpec(memory_space=pl.ANY)
    dma = pltpu.SemaphoreType.DMA
    return pl.pallas_call(
        functools.partial(kernel, R, C),
        out_shape=jax.ShapeDtypeStruct((rows, VIR), BF16),
        in_specs=[hbm] * 7,
        out_specs=pl.BlockSpec(memory_space=pltpu.VMEM),
        scratch_shapes=[
            pltpu.VMEM((occ_row, nd, sub, VIR), BF16),
            pltpu.VMEM(ladder.shape, BF16),
            pltpu.VMEM((1, VIR), F32),
            pltpu.VMEM((1, VIR), jnp.int32),
            pltpu.SMEM(occ_energy.shape, F32),
            pltpu.SMEM(occ_index.shape, jnp.int32),
            pltpu.VMEM((rows, VIR), BF16),
            pltpu.VMEM((R, depth, q_cols), BF16),
            pltpu.VMEM((R, Z, 2, chunk, q_cols), F32),
            pltpu.VMEM((R, Z, chunk, q_cols), F32),
            pltpu.VMEM((R, 2, chunk, q_cols), BF16),
            pltpu.VMEM((R, 2, chunk, q_cols), BF16),
            pltpu.VMEM((R, chunk, q_cols), BF16),
            pltpu.VMEM((R, chunk, q_cols), BF16),
            pltpu.VMEM((Z, 2, R, chunk, q_cols), BF16),
            pltpu.VMEM((R, occ_row, C, sub, VIR), BF16),
            pltpu.VMEM((R, occ_row, C, sub, VIR), BF16),
            pltpu.VMEM((occ_row, nd, sub, VIR), BF16),
            pltpu.VMEM((wide, wide), BF16),
            pltpu.VMEM((lad_rows, lad_cols), F32),
            pltpu.VMEM((nd, lad_rows, lad_cols), F32),
            pltpu.VMEM((rows, VIR), F32),
            pltpu.VMEM((4, chunk, VIR), F32),
            dma((8,)),
            dma((R,)), dma((R,)),
            dma((nd,)), dma((nd,)),
            dma((nd,)), dma((nd,)),
            dma((R,)), dma((R,)),
            dma((R,)), dma((R,)),
            dma((R,)), dma((R,)),
            dma((R,)), dma((R,)),
            dma((2, R)), dma((2, R)),
            dma((Z,)), dma((Z,)),
            dma((nd,)), dma((nd,)),
        ],
        compiler_params=pltpu.CompilerParams(
            collective_id=0, has_side_effects=True, vmem_limit_bytes=56 * 2**20
        ),
    )(
        amplitudes.reshape(occ_row, nd, sub, VIR), df_factors, ladder, occ_energy, occ_index,
        vir_energy.reshape(1, VIR), vir_map.reshape(1, VIR),
    )


def shards(amplitudes, df_factors, *rest):
    R, C = lax.axis_size("row"), lax.axis_size("col")
    rows, cols = amplitudes.shape
    fits = (
        VIR % (16 * R * C) == 0
        and cols == VIR
        and C == 8
        and rows % (16 * C) == 0
        and VIR % (rows // C) == 0
        and (rows // C) % (VIR // (R * C)) == 0
        and df_factors.shape[1] % 128 == 0
    )
    if fits:
        return fused(R, C, amplitudes, df_factors, *rest)
    return by_collectives(amplitudes, df_factors, *rest)


def solution(mesh):
    placed = (P("row", "col"), P("col", "row"), P(("row", "col"), None), P(), P(), P(), P())
    return jax.shard_map(
        shards, mesh=mesh, in_specs=placed, out_specs=P("row", "col"), check_vma=False
    )
```

```python
import functools

import jax
import jax.numpy as jnp
from jax import lax
from jax.experimental import pallas as pl
from jax.experimental.pallas import tpu as pltpu
from jax.sharding import PartitionSpec as P

VIR = 512
MESH = pl.DeviceIdType.MESH
F32 = jnp.float32
BF16 = jnp.bfloat16


def lookup(values, positions):
    table = jnp.arange(values.shape[0], dtype=jnp.int32)
    matches = positions[:, None] == table[None, :]
    return jnp.sum(jnp.where(matches, values[None, :], 0.0), axis=1)


def by_collectives(amplitudes, df_factors, ladder, occ_energy, occ_index, vir_energy, vir_map):
    rows_tile, cols_tile = amplitudes.shape
    occ_row = rows_tile // VIR
    occ_col = cols_tile // VIR
    occ_all = occ_index.shape[0]
    vir_rows = VIR // lax.axis_size("row")
    vir_cols = VIR // lax.axis_size("col")
    blocks = amplitudes.reshape(occ_row, VIR, occ_col, VIR)
    mirror = jnp.transpose(blocks, (0, 3, 2, 1))
    combined = (2.0 * blocks.astype(F32) - mirror.astype(F32)).astype(BF16)
    combined = combined.reshape(rows_tile, cols_tile)
    factors = lax.all_gather(df_factors, "row", axis=1, tiled=True)
    partial_fit = jnp.dot(combined, factors, preferred_element_type=F32)
    contract = (((1,), (1,)), ((), ()))
    shared = lax.psum_scatter(partial_fit, "col", scatter_dimension=1, tiled=True).astype(BF16)
    fitted = lax.all_gather(shared, "col", axis=1, tiled=True)
    coulomb = lax.dot_general(fitted, factors, contract, preferred_element_type=F32)
    arranged = lax.all_to_all(
        lax.all_to_all(blocks, "row", split_axis=1, concat_axis=0, tiled=True),
        "col",
        split_axis=3,
        concat_axis=2,
        tiled=True,
    )
    pair_major = jnp.transpose(arranged, (0, 2, 1, 3)).reshape(
        occ_all * occ_all, vir_rows * vir_cols
    )
    hole_wide = jnp.dot(
        lax.all_gather(ladder, ("row", "col"), axis=0, tiled=True),
        pair_major,
        preferred_element_type=F32,
    )
    hole_term = hole_wide.astype(BF16)
    returned = jnp.transpose(hole_term.reshape(occ_all, occ_all, vir_rows, vir_cols), (0, 2, 1, 3))
    hole_tile = lax.all_to_all(
        lax.all_to_all(returned, "row", split_axis=0, concat_axis=1, tiled=True),
        "col",
        split_axis=2,
        concat_axis=3,
        tiled=True,
    )
    row_start = lax.axis_index("row") * occ_row
    col_start = lax.axis_index("col") * occ_col
    row_energy = lookup(occ_energy, lax.dynamic_slice_in_dim(occ_index, row_start, occ_row))
    col_energy = lookup(occ_energy, lax.dynamic_slice_in_dim(occ_index, col_start, occ_col))
    virtual = lookup(vir_energy, vir_map)
    denominator = (
        row_energy[:, None, None, None]
        + col_energy[None, None, :, None]
        - virtual[None, :, None, None]
        - virtual[None, None, None, :]
    )
    summed = coulomb.reshape(occ_row, VIR, occ_col, VIR) + hole_tile.astype(F32)
    return (summed / denominator).astype(BF16).reshape(rows_tile, cols_tile)


def kernel(
    R, C, amp, fac, lad, occ_e, occ_i, vir_e, vir_m, out,
    amp_v, lad_v, e_v, m_v, occ_ev, occ_iv,
    comb, factors, part, twin, out1, in1, out2, in2, fit, pairs, hole, hole_in, kron, lad_own,
    lad_all, inverse, coul,
    loc, fac_s, fac_r, fwd_s, fwd_r, lad_s, lad_r, tw_s, tw_r, s1_s, s1_r, s2_s, s2_r,
    g1_s, g1_r, g2_s, g2_r, rl_s, rl_r, back_s, back_r,
):
    nd = R * C
    Z = C // 2
    occ_row, _, sub, _ = amp.shape
    rows = occ_row * VIR
    chunk = rows // C
    q_cols = fac.shape[1]
    per_pair = lad.shape[0]
    n_pairs = lad.shape[1]
    r = lax.axis_index("row")
    c = lax.axis_index("col")
    me = r * C + c
    core = lax.rem(c, 2)
    z = lax.div(c, 2)
    other = 1 - core
    near = z + 1 - 2 * lax.rem(z, 2)
    far = lax.rem(z + 2, Z)
    far_near = lax.rem(near + 2, Z)

    def place(d):
        return (lax.div(d, C), lax.rem(d, C))

    def peer(o):
        return lax.rem(r + lax.div(o, C), R) * C + lax.rem(c + lax.rem(o, C), C)

    def send(src, dst, s, d, target):
        return pltpu.make_async_remote_copy(
            src_ref=src, dst_ref=dst, send_sem=s, recv_sem=d, device_id=target, device_id_type=MESH
        )

    own_copies = [
        pltpu.make_async_copy(src, dst, loc.at[n])
        for n, (src, dst) in enumerate((
            (lad, lad_v), (amp, amp_v), (fac, factors.at[r]), (amp.at[:, me], pairs.at[r, :, c]),
            (vir_e, e_v), (vir_m, m_v), (occ_e, occ_ev), (occ_i, occ_iv),
        ))
    ]
    for copy in own_copies:
        copy.start()

    barrier = pltpu.get_barrier_semaphore()

    @pl.loop(1, nd)
    def _(o):
        pl.semaphore_signal(barrier, inc=1, device_id=place(peer(o)), device_id_type=MESH)

    lad_own[...] = jnp.zeros_like(lad_own)
    own_copies[0].wait()
    lad_own[0:per_pair, 0:n_pairs] = lad_v[...].astype(F32)
    lad_all[me] = lad_own[...]

    pl.semaphore_wait(barrier, nd - 1)

    def fac_copy(o):
        return send(
            fac, factors.at[r], fac_s.at[o], fac_r.at[r], (lax.rem(r + o, R), c)
        )

    for o in range(1, R):
        fac_copy(o).start()

    def fwd_copy(o):
        d = peer(o)
        return send(amp.at[:, d], pairs.at[r, :, c], fwd_s.at[o], fwd_r.at[me], place(d))

    def lad_copy(o):
        return send(lad_own, lad_all.at[me], lad_s.at[o], lad_r.at[me], place(peer(o)))

    def fwd_start(lo, hi):
        @pl.loop(lo, hi)
        def _(o):
            fwd_copy(o).start()

    fwd_start(1, C)

    own_copies[1].wait()
    for k in range(occ_row):
        slab = amp_v[k].reshape(VIR, VIR).astype(F32)
        comb[k * VIR:(k + 1) * VIR, :] = (2.0 * slab - slab.T).astype(BF16)
    own_copies[2].wait()

    def tw_copy(q):
        return send(part.at[q, :, other], twin.at[q], tw_s.at[q], tw_r.at[q], (r, 2 * z + other))

    def s1_copy(q):
        return send(out1.at[q], in1.at[q], s1_s.at[q], s1_r.at[q], (r, 2 * near + core))

    def s2_copy(q):
        return send(out2.at[q], in2.at[q], s2_s.at[q], s2_r.at[q], (r, 2 * far + core))

    def g1_copy(q):
        return send(
            fit.at[z, core, q], fit.at[z, core, q], g1_s.at[q], g1_r.at[q], (r, 2 * far + core)
        )

    def g2_copy(which, q):
        src = far if which else z
        return send(
            fit.at[src, core, q], fit.at[src, core, q], g2_s.at[which, q], g2_r.at[which, q],
            (r, 2 * near + core),
        )

    def relay(src):
        return send(
            fit.at[src, core], fit.at[src, core], rl_s.at[src], rl_r.at[src], (r, 2 * z + other)
        )

    order = [lax.rem(r + o, R) for o in range(R)]

    for o, q in enumerate(order):
        if o:
            send(fac, factors.at[q], fac_s.at[o], fac_r.at[q], (r, c)).wait_recv()
        got = jnp.dot(comb[...], factors[q], preferred_element_type=F32)
        part[q] = got.reshape(Z, 2, chunk, q_cols)
        tw_copy(q).start()
        if o == 0:
            fwd_start(C, nd)

            @pl.loop(1, nd)
            def _(n):
                lad_copy(n).start()

    for q in order:
        tw_copy(q).wait_recv()
        out1[q, 0] = (part[q, near, core] + twin[q, near]).astype(BF16)
        out1[q, 1] = (part[q, far_near, core] + twin[q, far_near]).astype(BF16)
        s1_copy(q).start()

    for copy in own_copies[4:]:
        copy.wait()
    ids_r = lax.broadcasted_iota(jnp.int32, (VIR, VIR), 0)
    ids_c = lax.broadcasted_iota(jnp.int32, (VIR, VIR), 1)
    e_col = jnp.sum(jnp.where(ids_r == ids_c, e_v[...], 0.0), axis=1, keepdims=True)
    v_row = jnp.sum(jnp.where(ids_r == m_v[...], e_col, 0.0), axis=0, keepdims=True)
    v_col = jnp.sum(jnp.where(ids_r == ids_c, v_row, 0.0), axis=1, keepdims=True)
    energy_j = occ_ev[occ_iv[c]]
    for k in range(occ_row):
        energy = occ_ev[occ_iv[r * occ_row + k]] + energy_j
        inverse[k * VIR:(k + 1) * VIR, :] = 1.0 / ((energy - v_col) - v_row)

    @pl.loop(1, nd)
    def _(o):
        d = peer(o)
        send(lad_own, lad_all.at[d], lad_s.at[o], lad_r.at[d], place(d)).wait_recv()

    shift = sub.bit_length() - 1
    wide = n_pairs * sub
    lad_flat = lad_all[...].reshape(nd * lad_own.shape[0], lad_own.shape[1]).astype(BF16)
    spread = (
        lax.broadcasted_iota(jnp.int32, (lad_own.shape[1], wide), 0)
        == (lax.broadcasted_iota(jnp.int32, (lad_own.shape[1], wide), 1) >> shift)
    )
    lad_wide = jnp.dot(
        lad_flat, spread.astype(F32).astype(BF16), preferred_element_type=F32
    ).astype(BF16)
    step_rows = 128

    @pl.loop(0, wide // step_rows)
    def _(n):
        at = pl.multiple_of(n * step_rows, step_rows)
        pair = (lax.broadcasted_iota(jnp.int32, (step_rows, lad_flat.shape[0]), 0) + at) >> shift
        held = lax.broadcasted_iota(jnp.int32, (step_rows, lad_flat.shape[0]), 1)
        pick = held == (lax.div(pair, per_pair) * lad_own.shape[0] + lax.rem(pair, per_pair))
        block = jnp.dot(pick.astype(F32).astype(BF16), lad_wide, preferred_element_type=F32)
        same = (lax.broadcasted_iota(jnp.int32, (step_rows, wide), 0) & (sub - 1)) == (
            lax.broadcasted_iota(jnp.int32, (step_rows, wide), 1) & (sub - 1)
        )
        kron[pl.ds(at, step_rows), :] = jnp.where(same, block, 0.0).astype(BF16)

    own_copies[3].wait()

    @pl.loop(1, nd)
    def _(o):
        d = peer(o)
        dr, dc = place(d)
        send(amp.at[:, d], pairs.at[dr, :, dc], fwd_s.at[o], fwd_r.at[d], (dr, dc)).wait_recv()

    row_blocks = wide // R
    for n in range(R):
        term = jnp.dot(
            kron[n * row_blocks:(n + 1) * row_blocks, :],
            pairs[...].reshape(wide, VIR),
            preferred_element_type=F32,
        )
        hole[n] = term.astype(BF16).reshape(occ_row, C, sub, VIR)

    def back_copy(o):
        d = peer(o)
        dr, dc = place(d)
        return send(hole.at[dr, :, dc], hole_in.at[:, me], back_s.at[o], back_r.at[me], (dr, dc))

    @pl.loop(1, nd)
    def _(o):
        back_copy(o).start()

    for q in order:
        s1_copy(q).wait_recv()
        out2[q] = ((part[q, far, core] + twin[q, far]) + in1[q, 1].astype(F32)).astype(BF16)
        s2_copy(q).start()

    hole_in[:, me] = hole[r, :, c]

    for q in order:
        s2_copy(q).wait_recv()
        total = (part[q, z, core] + twin[q, z]) + in1[q, 0].astype(F32)
        fit[z, core, q] = (total + in2[q].astype(F32)).astype(BF16)
        g1_copy(q).start()
        g2_copy(0, q).start()
    relay(z).start()

    def g1_wait(q):
        send(
            fit.at[far, core, q], fit.at[far, core, q], g1_s.at[q], g1_r.at[q], (r, c)
        ).wait_recv()

    def g2_wait(which, q):
        src = far_near if which else near
        send(
            fit.at[src, core, q], fit.at[src, core, q], g2_s.at[which, q], g2_r.at[which, q],
            (r, c),
        ).wait_recv()

    per_occ = VIR // chunk
    groups = chunk // sub

    def rows_of(n):
        return pl.ds(pl.multiple_of(n * chunk, chunk), chunk)

    def fitted_dot(src, which):
        acc = None
        for q in range(R):
            term = lax.dot_general(
                fit[src, which, q], factors[q], (((1,), (1,)), ((), ())),
                preferred_element_type=F32,
            )
            acc = term if acc is None else acc + term
        return acc

    def finish(src, which, acc):
        n = 2 * src + which
        k = lax.div(n, per_occ)
        m = lax.rem(n, per_occ)
        held = hole_in[k, pl.ds(m * groups, groups)].reshape(chunk, VIR).astype(F32)
        out[rows_of(n), :] = ((acc + held) * inverse[rows_of(n), :]).astype(BF16)

    def relay_wait(src):
        send(
            fit.at[src, other], fit.at[src, other], rl_s.at[src], rl_r.at[src], (r, c)
        ).wait_recv()

    coul[0] = fitted_dot(z, core)
    for q in order:
        g1_wait(q)
        g2_copy(1, q).start()
    relay(far).start()
    coul[1] = fitted_dot(far, core)
    relay_wait(z)
    coul[2] = fitted_dot(z, other)
    relay_wait(far)
    coul[3] = fitted_dot(far, other)

    @pl.loop(1, nd)
    def _(o):
        d = peer(o)
        send(hole.at[r, :, c], hole_in.at[:, d], back_s.at[o], back_r.at[d], place(d)).wait_recv()

    finish(z, core, coul[0])
    finish(far, core, coul[1])
    finish(z, other, coul[2])
    finish(far, other, coul[3])
    for which, src in ((0, near), (1, far_near)):
        for q in order:
            g2_wait(which, q)
        relay(src).start()
        finish(src, core, fitted_dot(src, core))
    for src in (near, far_near):
        relay_wait(src)
        finish(src, other, fitted_dot(src, other))

    @pl.loop(1, nd)
    def _(o):
        fwd_copy(o).wait_send()
        lad_copy(o).wait_send()
        back_copy(o).wait_send()

    for o in range(1, R):
        fac_copy(o).wait_send()
    for q in range(R):
        tw_copy(q).wait_send()
        s1_copy(q).wait_send()
        s2_copy(q).wait_send()
        g1_copy(q).wait_send()
        g2_copy(0, q).wait_send()
        g2_copy(1, q).wait_send()
    for o in range(Z):
        relay(o).wait_send()


def fused(R, C, amplitudes, df_factors, ladder, occ_energy, occ_index, vir_energy, vir_map):
    nd = R * C
    Z = C // 2
    rows, _ = amplitudes.shape
    occ_row = rows // VIR
    sub = VIR // nd
    chunk = rows // C
    depth, q_cols = df_factors.shape
    n_pairs = ladder.shape[1]
    wide = n_pairs * sub
    lad_rows = -(-ladder.shape[0] // 8) * 8
    lad_cols = -(-n_pairs // 128) * 128
    hbm = pl.BlockSpec(memory_space=pl.ANY)
    dma = pltpu.SemaphoreType.DMA
    return pl.pallas_call(
        functools.partial(kernel, R, C),
        out_shape=jax.ShapeDtypeStruct((rows, VIR), BF16),
        in_specs=[hbm] * 7,
        out_specs=pl.BlockSpec(memory_space=pltpu.VMEM),
        scratch_shapes=[
            pltpu.VMEM((occ_row, nd, sub, VIR), BF16),
            pltpu.VMEM(ladder.shape, BF16),
            pltpu.VMEM((1, VIR), F32),
            pltpu.VMEM((1, VIR), jnp.int32),
            pltpu.SMEM(occ_energy.shape, F32),
            pltpu.SMEM(occ_index.shape, jnp.int32),
            pltpu.VMEM((rows, VIR), BF16),
            pltpu.VMEM((R, depth, q_cols), BF16),
            pltpu.VMEM((R, Z, 2, chunk, q_cols), F32),
            pltpu.VMEM((R, Z, chunk, q_cols), F32),
            pltpu.VMEM((R, 2, chunk, q_cols), BF16),
            pltpu.VMEM((R, 2, chunk, q_cols), BF16),
            pltpu.VMEM((R, chunk, q_cols), BF16),
            pltpu.VMEM((R, chunk, q_cols), BF16),
            pltpu.VMEM((Z, 2, R, chunk, q_cols), BF16),
            pltpu.VMEM((R, occ_row, C, sub, VIR), BF16),
            pltpu.VMEM((R, occ_row, C, sub, VIR), BF16),
            pltpu.VMEM((occ_row, nd, sub, VIR), BF16),
            pltpu.VMEM((wide, wide), BF16),
            pltpu.VMEM((lad_rows, lad_cols), F32),
            pltpu.VMEM((nd, lad_rows, lad_cols), F32),
            pltpu.VMEM((rows, VIR), F32),
            pltpu.VMEM((4, chunk, VIR), F32),
            dma((8,)),
            dma((R,)), dma((R,)),
            dma((nd,)), dma((nd,)),
            dma((nd,)), dma((nd,)),
            dma((R,)), dma((R,)),
            dma((R,)), dma((R,)),
            dma((R,)), dma((R,)),
            dma((R,)), dma((R,)),
            dma((2, R)), dma((2, R)),
            dma((Z,)), dma((Z,)),
            dma((nd,)), dma((nd,)),
        ],
        compiler_params=pltpu.CompilerParams(
            collective_id=0, has_side_effects=True, vmem_limit_bytes=40 * 2**20
        ),
    )(
        amplitudes.reshape(occ_row, nd, sub, VIR), df_factors, ladder, occ_energy, occ_index,
        vir_energy.reshape(1, VIR), vir_map.reshape(1, VIR),
    )


def shards(amplitudes, df_factors, *rest):
    R, C = lax.axis_size("row"), lax.axis_size("col")
    rows, cols = amplitudes.shape
    fits = (
        VIR % (16 * R * C) == 0
        and cols == VIR
        and C == 8
        and rows % (16 * C) == 0
        and VIR % (rows // C) == 0
        and (rows // C) % (VIR // (R * C)) == 0
        and df_factors.shape[1] % 128 == 0
    )
    if fits:
        return fused(R, C, amplitudes, df_factors, *rest)
    return by_collectives(amplitudes, df_factors, *rest)


def solution(mesh):
    placed = (P("row", "col"), P("col", "row"), P(("row", "col"), None), P(), P(), P(), P())
    return jax.shard_map(
        shards, mesh=mesh, in_specs=placed, out_specs=P("row", "col"), check_vma=False
    )
```

```python
import functools

import jax
import jax.numpy as jnp
from jax import lax
from jax.experimental import pallas as pl
from jax.experimental.pallas import tpu as pltpu
from jax.sharding import PartitionSpec as P

VIR = 512
MESH = pl.DeviceIdType.MESH
F32 = jnp.float32
BF16 = jnp.bfloat16


def lookup(values, positions):
    table = jnp.arange(values.shape[0], dtype=jnp.int32)
    matches = positions[:, None] == table[None, :]
    return jnp.sum(jnp.where(matches, values[None, :], 0.0), axis=1)


def by_collectives(amplitudes, df_factors, ladder, occ_energy, occ_index, vir_energy, vir_map):
    rows_tile, cols_tile = amplitudes.shape
    occ_row = rows_tile // VIR
    occ_col = cols_tile // VIR
    occ_all = occ_index.shape[0]
    vir_rows = VIR // lax.axis_size("row")
    vir_cols = VIR // lax.axis_size("col")
    blocks = amplitudes.reshape(occ_row, VIR, occ_col, VIR)
    mirror = jnp.transpose(blocks, (0, 3, 2, 1))
    combined = (2.0 * blocks.astype(F32) - mirror.astype(F32)).astype(BF16)
    combined = combined.reshape(rows_tile, cols_tile)
    factors = lax.all_gather(df_factors, "row", axis=1, tiled=True)
    partial_fit = jnp.dot(combined, factors, preferred_element_type=F32)
    contract = (((1,), (1,)), ((), ()))
    shared = lax.psum_scatter(partial_fit, "col", scatter_dimension=1, tiled=True).astype(BF16)
    fitted = lax.all_gather(shared, "col", axis=1, tiled=True)
    coulomb = lax.dot_general(fitted, factors, contract, preferred_element_type=F32)
    arranged = lax.all_to_all(
        lax.all_to_all(blocks, "row", split_axis=1, concat_axis=0, tiled=True),
        "col",
        split_axis=3,
        concat_axis=2,
        tiled=True,
    )
    pair_major = jnp.transpose(arranged, (0, 2, 1, 3)).reshape(
        occ_all * occ_all, vir_rows * vir_cols
    )
    hole_wide = jnp.dot(
        lax.all_gather(ladder, ("row", "col"), axis=0, tiled=True),
        pair_major,
        preferred_element_type=F32,
    )
    hole_term = hole_wide.astype(BF16)
    returned = jnp.transpose(hole_term.reshape(occ_all, occ_all, vir_rows, vir_cols), (0, 2, 1, 3))
    hole_tile = lax.all_to_all(
        lax.all_to_all(returned, "row", split_axis=0, concat_axis=1, tiled=True),
        "col",
        split_axis=2,
        concat_axis=3,
        tiled=True,
    )
    row_start = lax.axis_index("row") * occ_row
    col_start = lax.axis_index("col") * occ_col
    row_energy = lookup(occ_energy, lax.dynamic_slice_in_dim(occ_index, row_start, occ_row))
    col_energy = lookup(occ_energy, lax.dynamic_slice_in_dim(occ_index, col_start, occ_col))
    virtual = lookup(vir_energy, vir_map)
    denominator = (
        row_energy[:, None, None, None]
        + col_energy[None, None, :, None]
        - virtual[None, :, None, None]
        - virtual[None, None, None, :]
    )
    summed = coulomb.reshape(occ_row, VIR, occ_col, VIR) + hole_tile.astype(F32)
    return (summed / denominator).astype(BF16).reshape(rows_tile, cols_tile)


def kernel(
    R, C, amp, fac, lad, occ_e, occ_i, vir_e, vir_m, out,
    amp_v, stage, lad_v, e_v, m_v, occ_ev, occ_iv,
    comb, factors, part, twin, out1, in1, out2, in2, fit, pairs, hole, hole_in, kron, lad_own,
    lad_all, inverse, coul,
    loc, fac_s, fac_r, fwd_s, fwd_r, hop_s, hop_r, lad_s, lad_r, tw_s, tw_r, s1_s, s1_r, s2_s, s2_r,
    g1_s, g1_r, g2_s, g2_r, rl_s, rl_r, back_s, back_r,
):
    nd = R * C
    Z = C // 2
    occ_row, _, _, sub, _ = amp.shape
    rows = occ_row * VIR
    chunk = rows // C
    q_cols = fac.shape[1]
    per_pair = lad.shape[0]
    n_pairs = lad.shape[1]
    r = lax.axis_index("row")
    c = lax.axis_index("col")
    me = r * C + c
    core = lax.rem(c, 2)
    z = lax.div(c, 2)
    other = 1 - core
    near = z + 1 - 2 * lax.rem(z, 2)
    far = lax.rem(z + 2, Z)
    far_near = lax.rem(near + 2, Z)

    def place(d):
        return (lax.div(d, C), lax.rem(d, C))

    def peer(o):
        return lax.rem(me + o, nd)

    def send(src, dst, s, d, target):
        return pltpu.make_async_remote_copy(
            src_ref=src, dst_ref=dst, send_sem=s, recv_sem=d, device_id=target, device_id_type=MESH
        )

    own_copies = [
        pltpu.make_async_copy(src, dst, loc.at[n])
        for n, (src, dst) in enumerate((
            (lad, lad_v), (amp, amp_v), (fac, factors.at[r]), (amp.at[:, r, c], pairs.at[r, :, c]),
            (vir_e, e_v), (vir_m, m_v), (occ_e, occ_ev), (occ_i, occ_iv),
        ))
    ]
    for copy in own_copies:
        copy.start()

    barrier = pltpu.get_barrier_semaphore()

    @pl.loop(1, nd)
    def _(o):
        pl.semaphore_signal(barrier, inc=1, device_id=place(peer(o)), device_id_type=MESH)

    lad_own[...] = jnp.zeros_like(lad_own)
    own_copies[0].wait()
    lad_own[0:per_pair, 0:n_pairs] = lad_v[...].astype(F32)
    lad_all[me] = lad_own[...]

    pl.semaphore_wait(barrier, nd - 1)

    order = [r, r + 1 - 2 * lax.rem(r, 2), lax.rem(r + 2, R), R - 1 - r]

    def fac_copy(o):
        return send(fac, factors.at[r], fac_s.at[o], fac_r.at[r], (order[o], c))

    for o in range(1, R):
        fac_copy(o).start()

    def col_peer(o):
        return lax.rem(c + o, C)

    def fwd_copy(o):
        to = col_peer(o)
        return send(amp.at[:, :, to], stage.at[c], fwd_s.at[o], fwd_r.at[c], (r, to))

    def hop_copy(src, o):
        return send(
            stage.at[src, :, order[o]], pairs.at[r, :, src], hop_s.at[o, src], hop_r.at[r, src],
            (order[o], c),
        )

    def own_hop_copy(o):
        return send(
            amp.at[:, order[o], c], pairs.at[r, :, c], hop_s.at[o, c], hop_r.at[r, c],
            (order[o], c),
        )

    def lad_copy(o):
        return send(lad_own, lad_all.at[me], lad_s.at[o], lad_r.at[me], place(peer(o)))

    for o in [C - 1, 1] + list(range(2, C - 1)):
        fwd_copy(o).start()

    own_copies[1].wait()
    for k in range(occ_row):
        slab = amp_v[k].reshape(VIR, VIR).astype(F32)
        comb[k * VIR:(k + 1) * VIR, :] = (2.0 * slab - slab.T).astype(BF16)
    own_copies[2].wait()

    def tw_copy(q):
        return send(part.at[q, :, other], twin.at[q], tw_s.at[q], tw_r.at[q], (r, 2 * z + other))

    def s1_copy(q):
        return send(out1.at[q], in1.at[q], s1_s.at[q], s1_r.at[q], (r, 2 * near + core))

    def s2_copy(q):
        return send(out2.at[q], in2.at[q], s2_s.at[q], s2_r.at[q], (r, 2 * far + core))

    def g1_copy(q):
        return send(
            fit.at[z, core, q], fit.at[z, core, q], g1_s.at[q], g1_r.at[q], (r, 2 * far + core)
        )

    def g2_copy(which, q):
        src = far if which else z
        return send(
            fit.at[src, core, q], fit.at[src, core, q], g2_s.at[which, q], g2_r.at[which, q],
            (r, 2 * near + core),
        )

    def relay(src):
        return send(
            fit.at[src, core], fit.at[src, core], rl_s.at[src], rl_r.at[src], (r, 2 * z + other)
        )

    def near_sums(q):
        tw_copy(q).wait_recv()
        out1[q, 0] = (part[q, near, core] + twin[q, near]).astype(BF16)
        out1[q, 1] = (part[q, far_near, core] + twin[q, far_near]).astype(BF16)
        s1_copy(q).start()

    for o, q in enumerate(order):
        if o:
            send(fac, factors.at[q], fac_s.at[o], fac_r.at[q], (r, c)).wait_recv()
        got = jnp.dot(comb[...], factors[q], preferred_element_type=F32)
        part[q] = got.reshape(Z, 2, chunk, q_cols)
        tw_copy(q).start()
        if o:
            near_sums(order[o - 1])
    for o in range(1, R):
        own_hop_copy(o).start()
    near_sums(order[R - 1])

    @pl.loop(1, nd)
    def _(n):
        lad_copy(n).start()

    @pl.loop(1, C)
    def _(n):
        src = lax.rem(c + n, C)
        send(
            amp.at[:, :, c], stage.at[src], fwd_s.at[n], fwd_r.at[src], (r, src)
        ).wait_recv()
        for o in range(1, R):
            hop_copy(src, o).start()
        pairs[r, :, src] = stage[src, :, r]

    for copy in own_copies[4:]:
        copy.wait()
    ids_r = lax.broadcasted_iota(jnp.int32, (VIR, VIR), 0)
    ids_c = lax.broadcasted_iota(jnp.int32, (VIR, VIR), 1)
    e_col = jnp.sum(jnp.where(ids_r == ids_c, e_v[...], 0.0), axis=1, keepdims=True)
    v_row = jnp.sum(jnp.where(ids_r == m_v[...], e_col, 0.0), axis=0, keepdims=True)
    v_col = jnp.sum(jnp.where(ids_r == ids_c, v_row, 0.0), axis=1, keepdims=True)
    energy_j = occ_ev[occ_iv[c]]
    for k in range(occ_row):
        energy = occ_ev[occ_iv[r * occ_row + k]] + energy_j
        inverse[k * VIR:(k + 1) * VIR, :] = 1.0 / ((energy - v_col) - v_row)

    @pl.loop(1, nd)
    def _(o):
        d = peer(o)
        send(lad_own, lad_all.at[d], lad_s.at[o], lad_r.at[d], place(d)).wait_recv()

    shift = sub.bit_length() - 1
    wide = n_pairs * sub
    lad_flat = lad_all[...].reshape(nd * lad_own.shape[0], lad_own.shape[1]).astype(BF16)
    spread = (
        lax.broadcasted_iota(jnp.int32, (lad_own.shape[1], wide), 0)
        == (lax.broadcasted_iota(jnp.int32, (lad_own.shape[1], wide), 1) >> shift)
    )
    lad_wide = jnp.dot(
        lad_flat, spread.astype(F32).astype(BF16), preferred_element_type=F32
    ).astype(BF16)
    step_rows = 128

    @pl.loop(0, wide // step_rows)
    def _(n):
        at = pl.multiple_of(n * step_rows, step_rows)
        pair = (lax.broadcasted_iota(jnp.int32, (step_rows, lad_flat.shape[0]), 0) + at) >> shift
        held = lax.broadcasted_iota(jnp.int32, (step_rows, lad_flat.shape[0]), 1)
        pick = held == (lax.div(pair, per_pair) * lad_own.shape[0] + lax.rem(pair, per_pair))
        block = jnp.dot(pick.astype(F32).astype(BF16), lad_wide, preferred_element_type=F32)
        same = (lax.broadcasted_iota(jnp.int32, (step_rows, wide), 0) & (sub - 1)) == (
            lax.broadcasted_iota(jnp.int32, (step_rows, wide), 1) & (sub - 1)
        )
        kron[pl.ds(at, step_rows), :] = jnp.where(same, block, 0.0).astype(BF16)

    for q in order:
        s1_copy(q).wait_recv()
        out2[q] = ((part[q, far, core] + twin[q, far]) + in1[q, 1].astype(F32)).astype(BF16)
        s2_copy(q).start()

    own_copies[3].wait()
    for o in range(1, R):
        @pl.loop(0, C)
        def _(src):
            send(
                stage.at[src, :, r], pairs.at[order[o], :, src], hop_s.at[o, src],
                hop_r.at[order[o], src], (order[o], c),
            ).wait_recv()

    row_blocks = wide // R
    for n in range(R):
        term = jnp.dot(
            kron[n * row_blocks:(n + 1) * row_blocks, :],
            pairs[...].reshape(wide, VIR),
            preferred_element_type=F32,
        )
        hole[n] = term.astype(BF16).reshape(occ_row, C, sub, VIR)

    def back_copy(o):
        d = peer(o)
        dr, dc = place(d)
        return send(hole.at[dr, :, dc], hole_in.at[:, me], back_s.at[o], back_r.at[me], (dr, dc))

    @pl.loop(1, nd // 2)
    def _(o):
        back_copy(o).start()

    hole_in[:, me] = hole[r, :, c]

    for q in order:
        s2_copy(q).wait_recv()
        total = (part[q, z, core] + twin[q, z]) + in1[q, 0].astype(F32)
        fit[z, core, q] = (total + in2[q].astype(F32)).astype(BF16)
        g1_copy(q).start()
        g2_copy(0, q).start()
    relay(z).start()

    @pl.loop(nd // 2, nd)
    def _(o):
        back_copy(o).start()


    def g1_wait(q):
        send(
            fit.at[far, core, q], fit.at[far, core, q], g1_s.at[q], g1_r.at[q], (r, c)
        ).wait_recv()

    def g2_wait(which, q):
        src = far_near if which else near
        send(
            fit.at[src, core, q], fit.at[src, core, q], g2_s.at[which, q], g2_r.at[which, q],
            (r, c),
        ).wait_recv()

    per_occ = VIR // chunk
    groups = chunk // sub

    def rows_of(n):
        return pl.ds(pl.multiple_of(n * chunk, chunk), chunk)

    def fitted_dot(src, which):
        acc = None
        for q in range(R):
            term = lax.dot_general(
                fit[src, which, q], factors[q], (((1,), (1,)), ((), ())),
                preferred_element_type=F32,
            )
            acc = term if acc is None else acc + term
        return acc

    def finish(src, which, acc):
        n = 2 * src + which
        k = lax.div(n, per_occ)
        m = lax.rem(n, per_occ)
        held = hole_in[k, pl.ds(m * groups, groups)].reshape(chunk, VIR).astype(F32)
        out[rows_of(n), :] = ((acc + held) * inverse[rows_of(n), :]).astype(BF16)

    def relay_wait(src):
        send(
            fit.at[src, other], fit.at[src, other], rl_s.at[src], rl_r.at[src], (r, c)
        ).wait_recv()

    coul[0] = fitted_dot(z, core)
    for q in order:
        g1_wait(q)
        g2_copy(1, q).start()
    relay(far).start()
    coul[1] = fitted_dot(far, core)
    relay_wait(z)
    coul[2] = fitted_dot(z, other)
    relay_wait(far)
    coul[3] = fitted_dot(far, other)

    @pl.loop(1, nd)
    def _(o):
        d = peer(o)
        send(hole.at[r, :, c], hole_in.at[:, d], back_s.at[o], back_r.at[d], place(d)).wait_recv()

    finish(z, core, coul[0])
    finish(far, core, coul[1])
    finish(z, other, coul[2])
    finish(far, other, coul[3])
    for which, src in ((0, near), (1, far_near)):
        for q in order:
            g2_wait(which, q)
        relay(src).start()
        finish(src, core, fitted_dot(src, core))
    for src in (near, far_near):
        relay_wait(src)
        finish(src, other, fitted_dot(src, other))

    @pl.loop(1, nd)
    def _(o):
        lad_copy(o).wait_send()
        back_copy(o).wait_send()

    for o in range(1, C):
        fwd_copy(o).wait_send()
    for o in range(1, R):
        fac_copy(o).wait_send()

        @pl.loop(0, C)
        def _(src):
            hop_copy(src, o).wait_send()
    for q in range(R):
        tw_copy(q).wait_send()
        s1_copy(q).wait_send()
        s2_copy(q).wait_send()
        g1_copy(q).wait_send()
        g2_copy(0, q).wait_send()
        g2_copy(1, q).wait_send()
    for o in range(Z):
        relay(o).wait_send()


def fused(R, C, amplitudes, df_factors, ladder, occ_energy, occ_index, vir_energy, vir_map):
    nd = R * C
    Z = C // 2
    rows, _ = amplitudes.shape
    occ_row = rows // VIR
    sub = VIR // nd
    chunk = rows // C
    depth, q_cols = df_factors.shape
    n_pairs = ladder.shape[1]
    wide = n_pairs * sub
    lad_rows = -(-ladder.shape[0] // 8) * 8
    lad_cols = -(-n_pairs // 128) * 128
    hbm = pl.BlockSpec(memory_space=pl.ANY)
    dma = pltpu.SemaphoreType.DMA
    return pl.pallas_call(
        functools.partial(kernel, R, C),
        out_shape=jax.ShapeDtypeStruct((rows, VIR), BF16),
        in_specs=[hbm] * 7,
        out_specs=pl.BlockSpec(memory_space=pltpu.VMEM),
        scratch_shapes=[
            pltpu.VMEM((occ_row, R, C, sub, VIR), BF16),
            pltpu.VMEM((C, occ_row, R, sub, VIR), BF16),
            pltpu.VMEM(ladder.shape, BF16),
            pltpu.VMEM((1, VIR), F32),
            pltpu.VMEM((1, VIR), jnp.int32),
            pltpu.SMEM(occ_energy.shape, F32),
            pltpu.SMEM(occ_index.shape, jnp.int32),
            pltpu.VMEM((rows, VIR), BF16),
            pltpu.VMEM((R, depth, q_cols), BF16),
            pltpu.VMEM((R, Z, 2, chunk, q_cols), F32),
            pltpu.VMEM((R, Z, chunk, q_cols), F32),
            pltpu.VMEM((R, 2, chunk, q_cols), BF16),
            pltpu.VMEM((R, 2, chunk, q_cols), BF16),
            pltpu.VMEM((R, chunk, q_cols), BF16),
            pltpu.VMEM((R, chunk, q_cols), BF16),
            pltpu.VMEM((Z, 2, R, chunk, q_cols), BF16),
            pltpu.VMEM((R, occ_row, C, sub, VIR), BF16),
            pltpu.VMEM((R, occ_row, C, sub, VIR), BF16),
            pltpu.VMEM((occ_row, nd, sub, VIR), BF16),
            pltpu.VMEM((wide, wide), BF16),
            pltpu.VMEM((lad_rows, lad_cols), F32),
            pltpu.VMEM((nd, lad_rows, lad_cols), F32),
            pltpu.VMEM((rows, VIR), F32),
            pltpu.VMEM((4, chunk, VIR), F32),
            dma((8,)),
            dma((R,)), dma((R,)),
            dma((C,)), dma((C,)),
            dma((R, C)), dma((R, C)),
            dma((nd,)), dma((nd,)),
            dma((R,)), dma((R,)),
            dma((R,)), dma((R,)),
            dma((R,)), dma((R,)),
            dma((R,)), dma((R,)),
            dma((2, R)), dma((2, R)),
            dma((Z,)), dma((Z,)),
            dma((nd,)), dma((nd,)),
        ],
        compiler_params=pltpu.CompilerParams(
            collective_id=0, has_side_effects=True, vmem_limit_bytes=56 * 2**20
        ),
    )(
        amplitudes.reshape(occ_row, R, C, sub, VIR), df_factors, ladder, occ_energy, occ_index,
        vir_energy.reshape(1, VIR), vir_map.reshape(1, VIR),
    )


def shards(amplitudes, df_factors, *rest):
    R, C = lax.axis_size("row"), lax.axis_size("col")
    rows, cols = amplitudes.shape
    fits = (
        VIR % (16 * R * C) == 0
        and cols == VIR
        and (R, C) == (4, 8)
        and rows % (16 * C) == 0
        and VIR % (rows // C) == 0
        and (rows // C) % (VIR // (R * C)) == 0
        and df_factors.shape[1] % 128 == 0
    )
    if fits:
        return fused(R, C, amplitudes, df_factors, *rest)
    return by_collectives(amplitudes, df_factors, *rest)


def solution(mesh):
    placed = (P("row", "col"), P("col", "row"), P(("row", "col"), None), P(), P(), P(), P())
    return jax.shard_map(
        shards, mesh=mesh, in_specs=placed, out_specs=P("row", "col"), check_vma=False
    )
```

```python
import functools

import jax
import jax.numpy as jnp
from jax import lax
from jax.experimental import pallas as pl
from jax.experimental.pallas import tpu as pltpu
from jax.sharding import PartitionSpec as P

VIR = 512
MESH = pl.DeviceIdType.MESH
F32 = jnp.float32
BF16 = jnp.bfloat16


def lookup(values, positions):
    table = jnp.arange(values.shape[0], dtype=jnp.int32)
    matches = positions[:, None] == table[None, :]
    return jnp.sum(jnp.where(matches, values[None, :], 0.0), axis=1)


def by_collectives(amplitudes, df_factors, ladder, occ_energy, occ_index, vir_energy, vir_map):
    rows_tile, cols_tile = amplitudes.shape
    occ_row = rows_tile // VIR
    occ_col = cols_tile // VIR
    occ_all = occ_index.shape[0]
    vir_rows = VIR // lax.axis_size("row")
    vir_cols = VIR // lax.axis_size("col")
    blocks = amplitudes.reshape(occ_row, VIR, occ_col, VIR)
    mirror = jnp.transpose(blocks, (0, 3, 2, 1))
    combined = (2.0 * blocks.astype(F32) - mirror.astype(F32)).astype(BF16)
    combined = combined.reshape(rows_tile, cols_tile)
    factors = lax.all_gather(df_factors, "row", axis=1, tiled=True)
    partial_fit = jnp.dot(combined, factors, preferred_element_type=F32)
    contract = (((1,), (1,)), ((), ()))
    shared = lax.psum_scatter(partial_fit, "col", scatter_dimension=1, tiled=True).astype(BF16)
    fitted = lax.all_gather(shared, "col", axis=1, tiled=True)
    coulomb = lax.dot_general(fitted, factors, contract, preferred_element_type=F32)
    arranged = lax.all_to_all(
        lax.all_to_all(blocks, "row", split_axis=1, concat_axis=0, tiled=True),
        "col",
        split_axis=3,
        concat_axis=2,
        tiled=True,
    )
    pair_major = jnp.transpose(arranged, (0, 2, 1, 3)).reshape(
        occ_all * occ_all, vir_rows * vir_cols
    )
    hole_wide = jnp.dot(
        lax.all_gather(ladder, ("row", "col"), axis=0, tiled=True),
        pair_major,
        preferred_element_type=F32,
    )
    hole_term = hole_wide.astype(BF16)
    returned = jnp.transpose(hole_term.reshape(occ_all, occ_all, vir_rows, vir_cols), (0, 2, 1, 3))
    hole_tile = lax.all_to_all(
        lax.all_to_all(returned, "row", split_axis=0, concat_axis=1, tiled=True),
        "col",
        split_axis=2,
        concat_axis=3,
        tiled=True,
    )
    row_start = lax.axis_index("row") * occ_row
    col_start = lax.axis_index("col") * occ_col
    row_energy = lookup(occ_energy, lax.dynamic_slice_in_dim(occ_index, row_start, occ_row))
    col_energy = lookup(occ_energy, lax.dynamic_slice_in_dim(occ_index, col_start, occ_col))
    virtual = lookup(vir_energy, vir_map)
    denominator = (
        row_energy[:, None, None, None]
        + col_energy[None, None, :, None]
        - virtual[None, :, None, None]
        - virtual[None, None, None, :]
    )
    summed = coulomb.reshape(occ_row, VIR, occ_col, VIR) + hole_tile.astype(F32)
    return (summed / denominator).astype(BF16).reshape(rows_tile, cols_tile)


def kernel(
    R, C, amp, fac, lad, occ_e, occ_i, vir_e, vir_m, out,
    amp_v, lad_v, e_v, m_v, occ_ev, occ_iv,
    comb, factors, turned, part, away, twin, out1, in1, out2, in2, fit, pairs, hole, hole_in, kron, lad_own,
    lad_all, inverse, coul,
    loc, fac_s, fac_r, fwd_s, fwd_r, lad_s, lad_r, tw_s, tw_r, s1_s, s1_r, s2_s, s2_r,
    g1_s, g1_r, g2_s, g2_r, rl_s, rl_r, back_s, back_r,
):
    nd = R * C
    Z = C // 2
    occ_row, _, sub, _ = amp.shape
    rows = occ_row * VIR
    chunk = rows // C
    q_cols = fac.shape[1]
    per_pair = lad.shape[0]
    n_pairs = lad.shape[1]
    r = lax.axis_index("row")
    c = lax.axis_index("col")
    me = r * C + c
    core = lax.rem(c, 2)
    z = lax.div(c, 2)
    other = 1 - core
    near = z + 1 - 2 * lax.rem(z, 2)
    far = lax.rem(z + 2, Z)
    far_near = lax.rem(near + 2, Z)

    def place(d):
        return (lax.div(d, C), lax.rem(d, C))

    def peer(o):
        return lax.rem(me + o, nd)

    def send(src, dst, s, d, target):
        return pltpu.make_async_remote_copy(
            src_ref=src, dst_ref=dst, send_sem=s, recv_sem=d, device_id=target, device_id_type=MESH
        )

    own_copies = [
        pltpu.make_async_copy(src, dst, loc.at[n])
        for n, (src, dst) in enumerate((
            (lad, lad_v), (amp, amp_v), (fac, factors.at[r]), (amp.at[:, me], pairs.at[r, :, c]),
            (vir_e, e_v), (vir_m, m_v), (occ_e, occ_ev), (occ_i, occ_iv),
        ))
    ]
    for copy in own_copies:
        copy.start()

    barrier = pltpu.get_barrier_semaphore()

    @pl.loop(1, nd)
    def _(o):
        pl.semaphore_signal(barrier, inc=1, device_id=place(peer(o)), device_id_type=MESH)

    lad_own[...] = jnp.zeros_like(lad_own)
    own_copies[0].wait()
    lad_own[0:per_pair, 0:n_pairs] = lad_v[...].astype(F32)
    lad_all[me] = lad_own[...]

    pl.semaphore_wait(barrier, nd - 1)

    order = [r, r + 1 - 2 * lax.rem(r, 2), lax.rem(r + 2, R), R - 1 - r]

    def fac_copy(o):
        return send(fac, factors.at[r], fac_s.at[o], fac_r.at[r], (order[o], c))

    for o in range(1, R):
        fac_copy(o).start()

    def fwd_copy(o):
        d = peer(o)
        return send(amp.at[:, d], pairs.at[r, :, c], fwd_s.at[o], fwd_r.at[me], place(d))

    def lad_copy(o):
        return send(lad_own, lad_all.at[me], lad_s.at[o], lad_r.at[me], place(peer(o)))

    def fwd_start(lo, hi):
        @pl.loop(lo, hi)
        def _(o):
            fwd_copy(o).start()

    @pl.loop(1, nd)
    def _(n):
        lad_copy(n).start()

    fwd_start(1, nd)

    own_copies[1].wait()
    for k in range(occ_row):
        slab = amp_v[k].reshape(VIR, VIR).astype(F32)
        comb[k * VIR:(k + 1) * VIR, :] = (2.0 * slab - slab.T).astype(BF16)
    own_copies[2].wait()

    def tw_copy(q):
        return send(away.at[q], twin.at[q], tw_s.at[q], tw_r.at[q], (r, 2 * z + other))

    def s1_copy(q):
        return send(out1.at[q], in1.at[q], s1_s.at[q], s1_r.at[q], (r, 2 * near + core))

    def s2_copy(q):
        return send(out2.at[q], in2.at[q], s2_s.at[q], s2_r.at[q], (r, 2 * far + core))

    def g1_copy(q):
        return send(
            fit.at[z, core, q], fit.at[z, core, q], g1_s.at[q], g1_r.at[q], (r, 2 * far + core)
        )

    def g2_copy(which, q):
        src = far if which else z
        return send(
            fit.at[src, core, q], fit.at[src, core, q], g2_s.at[which, q], g2_r.at[which, q],
            (r, 2 * near + core),
        )

    def relay(src):
        return send(
            fit.at[src, core], fit.at[src, core], rl_s.at[src], rl_r.at[src], (r, 2 * z + other)
        )

    def partial_sums(q):
        got = jnp.dot(comb[...], factors[q], preferred_element_type=F32)
        got = got.reshape(Z, 2, chunk, q_cols)
        part[q] = got
        away[q] = part[q, :, other].astype(BF16)
        tw_copy(q).start()

    def pair_sum(q, to):
        return part[q, to, core] + twin[q, to].astype(F32)

    def near_sums(q):
        tw_copy(q).wait_recv()
        out1[q, 0] = pair_sum(q, near).astype(BF16)
        out1[q, 1] = pair_sum(q, far_near).astype(BF16)
        s1_copy(q).start()

    partial_sums(r)

    for copy in own_copies[4:]:
        copy.wait()
    ids_r = lax.broadcasted_iota(jnp.int32, (VIR, VIR), 0)
    ids_c = lax.broadcasted_iota(jnp.int32, (VIR, VIR), 1)
    e_col = jnp.sum(jnp.where(ids_r == ids_c, e_v[...], 0.0), axis=1, keepdims=True)
    v_row = jnp.sum(jnp.where(ids_r == m_v[...], e_col, 0.0), axis=0, keepdims=True)
    v_col = jnp.sum(jnp.where(ids_r == ids_c, v_row, 0.0), axis=1, keepdims=True)
    energy_j = occ_ev[occ_iv[c]]
    for k in range(occ_row):
        energy = occ_ev[occ_iv[r * occ_row + k]] + energy_j
        inverse[k * VIR:(k + 1) * VIR, :] = 1.0 / ((energy - v_col) - v_row)

    near_sums(r)

    @pl.loop(1, nd)
    def _(o):
        d = peer(o)
        send(lad_own, lad_all.at[d], lad_s.at[o], lad_r.at[d], place(d)).wait_recv()

    shift = sub.bit_length() - 1
    wide = n_pairs * sub
    lad_flat = lad_all[...].reshape(nd * lad_own.shape[0], lad_own.shape[1]).astype(BF16)
    spread = (
        lax.broadcasted_iota(jnp.int32, (lad_own.shape[1], wide), 0)
        == (lax.broadcasted_iota(jnp.int32, (lad_own.shape[1], wide), 1) >> shift)
    )
    lad_wide = jnp.dot(
        lad_flat, spread.astype(F32).astype(BF16), preferred_element_type=F32
    ).astype(BF16)
    step_rows = 128

    @pl.loop(0, wide // step_rows)
    def _(n):
        at = pl.multiple_of(n * step_rows, step_rows)
        pair = (lax.broadcasted_iota(jnp.int32, (step_rows, lad_flat.shape[0]), 0) + at) >> shift
        held = lax.broadcasted_iota(jnp.int32, (step_rows, lad_flat.shape[0]), 1)
        pick = held == (lax.div(pair, per_pair) * lad_own.shape[0] + lax.rem(pair, per_pair))
        block = jnp.dot(pick.astype(F32).astype(BF16), lad_wide, preferred_element_type=F32)
        same = (lax.broadcasted_iota(jnp.int32, (step_rows, wide), 0) & (sub - 1)) == (
            lax.broadcasted_iota(jnp.int32, (step_rows, wide), 1) & (sub - 1)
        )
        kron[pl.ds(at, step_rows), :] = jnp.where(same, block, 0.0).astype(BF16)

    for o in range(1, R):
        q = order[o]
        send(fac, factors.at[q], fac_s.at[o], fac_r.at[q], (r, c)).wait_recv()
        partial_sums(q)
        if o > 1:
            near_sums(order[o - 1])
    near_sums(order[R - 1])

    for q in range(R):
        turned[q] = factors[q].T

    for q in order:
        s1_copy(q).wait_recv()
        out2[q] = (pair_sum(q, far) + in1[q, 1].astype(F32)).astype(BF16)
        s2_copy(q).start()

    own_copies[3].wait()

    @pl.loop(1, nd)
    def _(o):
        d = peer(o)
        dr, dc = place(d)
        send(amp.at[:, d], pairs.at[dr, :, dc], fwd_s.at[o], fwd_r.at[d], (dr, dc)).wait_recv()

    row_blocks = wide // R
    for n in range(R):
        term = jnp.dot(
            kron[n * row_blocks:(n + 1) * row_blocks, :],
            pairs[...].reshape(wide, VIR),
            preferred_element_type=F32,
        )
        hole[n] = term.astype(BF16).reshape(occ_row, C, sub, VIR)

    def back_copy(o):
        d = peer(o)
        dr, dc = place(d)
        return send(hole.at[dr, :, dc], hole_in.at[:, me], back_s.at[o], back_r.at[me], (dr, dc))

    @pl.loop(1, nd // 2)
    def _(o):
        back_copy(o).start()

    hole_in[:, me] = hole[r, :, c]

    for q in order:
        s2_copy(q).wait_recv()
        total = pair_sum(q, z) + in1[q, 0].astype(F32)
        fit[z, core, q] = (total + in2[q].astype(F32)).astype(BF16)
        g1_copy(q).start()
        g2_copy(0, q).start()
    relay(z).start()

    @pl.loop(nd // 2, nd)
    def _(o):
        back_copy(o).start()

    def g1_wait(q):
        send(
            fit.at[far, core, q], fit.at[far, core, q], g1_s.at[q], g1_r.at[q], (r, c)
        ).wait_recv()

    def g2_wait(which, q):
        src = far_near if which else near
        send(
            fit.at[src, core, q], fit.at[src, core, q], g2_s.at[which, q], g2_r.at[which, q],
            (r, c),
        ).wait_recv()

    per_occ = VIR // chunk
    groups = chunk // sub

    def rows_of(n):
        return pl.ds(pl.multiple_of(n * chunk, chunk), chunk)

    def fitted_dot(src, which):
        acc = None
        for q in range(R):
            term = jnp.dot(fit[src, which, q], turned[q], preferred_element_type=F32)
            acc = term if acc is None else acc + term
        return acc

    def finish(src, which, acc):
        n = 2 * src + which
        k = lax.div(n, per_occ)
        m = lax.rem(n, per_occ)
        held = hole_in[k, pl.ds(m * groups, groups)].reshape(chunk, VIR).astype(F32)
        out[rows_of(n), :] = ((acc + held) * inverse[rows_of(n), :]).astype(BF16)

    def relay_wait(src):
        send(
            fit.at[src, other], fit.at[src, other], rl_s.at[src], rl_r.at[src], (r, c)
        ).wait_recv()

    coul[0] = fitted_dot(z, core)
    for q in order:
        g1_wait(q)
        g2_copy(1, q).start()
    relay(far).start()
    coul[1] = fitted_dot(far, core)
    relay_wait(z)
    coul[2] = fitted_dot(z, other)
    relay_wait(far)
    coul[3] = fitted_dot(far, other)

    @pl.loop(1, nd)
    def _(o):
        d = peer(o)
        send(hole.at[r, :, c], hole_in.at[:, d], back_s.at[o], back_r.at[d], place(d)).wait_recv()

    finish(z, core, coul[0])
    finish(far, core, coul[1])
    finish(z, other, coul[2])
    finish(far, other, coul[3])
    for which, src in ((0, near), (1, far_near)):
        for q in order:
            g2_wait(which, q)
        relay(src).start()
        finish(src, core, fitted_dot(src, core))
    for src in (near, far_near):
        relay_wait(src)
        finish(src, other, fitted_dot(src, other))

    @pl.loop(1, nd)
    def _(o):
        fwd_copy(o).wait_send()
        lad_copy(o).wait_send()
        back_copy(o).wait_send()

    for o in range(1, R):
        fac_copy(o).wait_send()
    for q in range(R):
        tw_copy(q).wait_send()
        s1_copy(q).wait_send()
        s2_copy(q).wait_send()
        g1_copy(q).wait_send()
        g2_copy(0, q).wait_send()
        g2_copy(1, q).wait_send()
    for o in range(Z):
        relay(o).wait_send()


def fused(R, C, amplitudes, df_factors, ladder, occ_energy, occ_index, vir_energy, vir_map):
    nd = R * C
    Z = C // 2
    rows, _ = amplitudes.shape
    occ_row = rows // VIR
    sub = VIR // nd
    chunk = rows // C
    depth, q_cols = df_factors.shape
    n_pairs = ladder.shape[1]
    wide = n_pairs * sub
    lad_rows = -(-ladder.shape[0] // 8) * 8
    lad_cols = -(-n_pairs // 128) * 128
    hbm = pl.BlockSpec(memory_space=pl.ANY)
    dma = pltpu.SemaphoreType.DMA
    return pl.pallas_call(
        functools.partial(kernel, R, C),
        out_shape=jax.ShapeDtypeStruct((rows, VIR), BF16),
        in_specs=[hbm] * 7,
        out_specs=pl.BlockSpec(memory_space=pltpu.VMEM),
        scratch_shapes=[
            pltpu.VMEM((occ_row, nd, sub, VIR), BF16),
            pltpu.VMEM(ladder.shape, BF16),
            pltpu.VMEM((1, VIR), F32),
            pltpu.VMEM((1, VIR), jnp.int32),
            pltpu.SMEM(occ_energy.shape, F32),
            pltpu.SMEM(occ_index.shape, jnp.int32),
            pltpu.VMEM((rows, VIR), BF16),
            pltpu.VMEM((R, depth, q_cols), BF16),
            pltpu.VMEM((R, q_cols, depth), BF16),
            pltpu.VMEM((R, Z, 2, chunk, q_cols), F32),
            pltpu.VMEM((R, Z, chunk, q_cols), BF16),
            pltpu.VMEM((R, Z, chunk, q_cols), BF16),
            pltpu.VMEM((R, 2, chunk, q_cols), BF16),
            pltpu.VMEM((R, 2, chunk, q_cols), BF16),
            pltpu.VMEM((R, chunk, q_cols), BF16),
            pltpu.VMEM((R, chunk, q_cols), BF16),
            pltpu.VMEM((Z, 2, R, chunk, q_cols), BF16),
            pltpu.VMEM((R, occ_row, C, sub, VIR), BF16),
            pltpu.VMEM((R, occ_row, C, sub, VIR), BF16),
            pltpu.VMEM((occ_row, nd, sub, VIR), BF16),
            pltpu.VMEM((wide, wide), BF16),
            pltpu.VMEM((lad_rows, lad_cols), F32),
            pltpu.VMEM((nd, lad_rows, lad_cols), F32),
            pltpu.VMEM((rows, VIR), F32),
            pltpu.VMEM((4, chunk, VIR), F32),
            dma((8,)),
            dma((R,)), dma((R,)),
            dma((nd,)), dma((nd,)),
            dma((nd,)), dma((nd,)),
            dma((R,)), dma((R,)),
            dma((R,)), dma((R,)),
            dma((R,)), dma((R,)),
            dma((R,)), dma((R,)),
            dma((2, R)), dma((2, R)),
            dma((Z,)), dma((Z,)),
            dma((nd,)), dma((nd,)),
        ],
        compiler_params=pltpu.CompilerParams(
            collective_id=0, has_side_effects=True, vmem_limit_bytes=56 * 2**20
        ),
    )(
        amplitudes.reshape(occ_row, nd, sub, VIR), df_factors, ladder, occ_energy, occ_index,
        vir_energy.reshape(1, VIR), vir_map.reshape(1, VIR),
    )


def shards(amplitudes, df_factors, *rest):
    R, C = lax.axis_size("row"), lax.axis_size("col")
    rows, cols = amplitudes.shape
    fits = (
        VIR % (16 * R * C) == 0
        and cols == VIR
        and (R, C) == (4, 8)
        and rows % (16 * C) == 0
        and VIR % (rows // C) == 0
        and (rows // C) % (VIR // (R * C)) == 0
        and df_factors.shape[1] % 128 == 0
    )
    if fits:
        return fused(R, C, amplitudes, df_factors, *rest)
    return by_collectives(amplitudes, df_factors, *rest)


def solution(mesh):
    placed = (P("row", "col"), P("col", "row"), P(("row", "col"), None), P(), P(), P(), P())
    return jax.shard_map(
        shards, mesh=mesh, in_specs=placed, out_specs=P("row", "col"), check_vma=False
    )
```

```python
import functools

import jax
import jax.numpy as jnp
from jax import lax
from jax.experimental import pallas as pl
from jax.experimental.pallas import tpu as pltpu
from jax.sharding import PartitionSpec as P

VIR = 512
MESH = pl.DeviceIdType.MESH
F32 = jnp.float32
BF16 = jnp.bfloat16


def lookup(values, positions):
    table = jnp.arange(values.shape[0], dtype=jnp.int32)
    matches = positions[:, None] == table[None, :]
    return jnp.sum(jnp.where(matches, values[None, :], 0.0), axis=1)


def by_collectives(amplitudes, df_factors, ladder, occ_energy, occ_index, vir_energy, vir_map):
    rows_tile, cols_tile = amplitudes.shape
    occ_row = rows_tile // VIR
    occ_col = cols_tile // VIR
    occ_all = occ_index.shape[0]
    vir_rows = VIR // lax.axis_size("row")
    vir_cols = VIR // lax.axis_size("col")
    blocks = amplitudes.reshape(occ_row, VIR, occ_col, VIR)
    mirror = jnp.transpose(blocks, (0, 3, 2, 1))
    combined = (2.0 * blocks.astype(F32) - mirror.astype(F32)).astype(BF16)
    combined = combined.reshape(rows_tile, cols_tile)
    factors = lax.all_gather(df_factors, "row", axis=1, tiled=True)
    partial_fit = jnp.dot(combined, factors, preferred_element_type=F32)
    contract = (((1,), (1,)), ((), ()))
    shared = lax.psum_scatter(partial_fit, "col", scatter_dimension=1, tiled=True).astype(BF16)
    fitted = lax.all_gather(shared, "col", axis=1, tiled=True)
    coulomb = lax.dot_general(fitted, factors, contract, preferred_element_type=F32)
    arranged = lax.all_to_all(
        lax.all_to_all(blocks, "row", split_axis=1, concat_axis=0, tiled=True),
        "col",
        split_axis=3,
        concat_axis=2,
        tiled=True,
    )
    pair_major = jnp.transpose(arranged, (0, 2, 1, 3)).reshape(
        occ_all * occ_all, vir_rows * vir_cols
    )
    hole_wide = jnp.dot(
        lax.all_gather(ladder, ("row", "col"), axis=0, tiled=True),
        pair_major,
        preferred_element_type=F32,
    )
    hole_term = hole_wide.astype(BF16)
    returned = jnp.transpose(hole_term.reshape(occ_all, occ_all, vir_rows, vir_cols), (0, 2, 1, 3))
    hole_tile = lax.all_to_all(
        lax.all_to_all(returned, "row", split_axis=0, concat_axis=1, tiled=True),
        "col",
        split_axis=2,
        concat_axis=3,
        tiled=True,
    )
    row_start = lax.axis_index("row") * occ_row
    col_start = lax.axis_index("col") * occ_col
    row_energy = lookup(occ_energy, lax.dynamic_slice_in_dim(occ_index, row_start, occ_row))
    col_energy = lookup(occ_energy, lax.dynamic_slice_in_dim(occ_index, col_start, occ_col))
    virtual = lookup(vir_energy, vir_map)
    denominator = (
        row_energy[:, None, None, None]
        + col_energy[None, None, :, None]
        - virtual[None, :, None, None]
        - virtual[None, None, None, :]
    )
    summed = coulomb.reshape(occ_row, VIR, occ_col, VIR) + hole_tile.astype(F32)
    return (summed / denominator).astype(BF16).reshape(rows_tile, cols_tile)


def kernel(
    R, C, amp, fac, lad, occ_e, occ_i, vir_e, vir_m, out,
    amp_v, lad_v, e_v, m_v, occ_ev, occ_iv,
    comb, factors, turned, part, away, twin, out1, in1, out2, in2, fit, pairs, hole, hole_in, kron, lad_own,
    lad_all, inverse, coul, held_sum,
    loc, fac_s, fac_r, fwd_s, fwd_r, lad_s, lad_r, tw_s, tw_r, s1_s, s1_r, s2_s, s2_r,
    g1_s, g1_r, g2_s, g2_r, rl_s, rl_r, back_s, back_r,
):
    nd = R * C
    Z = C // 2
    occ_row, _, sub, _ = amp.shape
    rows = occ_row * VIR
    chunk = rows // C
    q_cols = fac.shape[1]
    per_pair = lad.shape[0]
    n_pairs = lad.shape[1]
    r = lax.axis_index("row")
    c = lax.axis_index("col")
    me = r * C + c
    core = lax.rem(c, 2)
    z = lax.div(c, 2)
    other = 1 - core
    near = z + 1 - 2 * lax.rem(z, 2)
    far = lax.rem(z + 2, Z)
    far_near = lax.rem(near + 2, Z)

    def place(d):
        return (lax.div(d, C), lax.rem(d, C))

    def peer(o):
        return lax.rem(me + o, nd)

    def send(src, dst, s, d, target):
        return pltpu.make_async_remote_copy(
            src_ref=src, dst_ref=dst, send_sem=s, recv_sem=d, device_id=target, device_id_type=MESH
        )

    own_copies = [
        pltpu.make_async_copy(src, dst, loc.at[n])
        for n, (src, dst) in enumerate((
            (lad, lad_v), (amp, amp_v), (fac, factors.at[r]), (amp.at[:, me], pairs.at[r, :, c]),
            (vir_e, e_v), (vir_m, m_v), (occ_e, occ_ev), (occ_i, occ_iv),
        ))
    ]
    for copy in own_copies:
        copy.start()

    barrier = pltpu.get_barrier_semaphore()

    @pl.loop(1, nd)
    def _(o):
        pl.semaphore_signal(barrier, inc=1, device_id=place(peer(o)), device_id_type=MESH)

    lad_own[...] = jnp.zeros_like(lad_own)
    own_copies[0].wait()
    lad_own[0:per_pair, 0:n_pairs] = lad_v[...].astype(F32)
    lad_all[me] = lad_own[...]

    pl.semaphore_wait(barrier, nd - 1)

    order = [r, r + 1 - 2 * lax.rem(r, 2), lax.rem(r + 2, R), R - 1 - r]

    def fac_copy(o):
        return send(fac, factors.at[r], fac_s.at[o], fac_r.at[r], (order[o], c))

    for o in range(1, R):
        fac_copy(o).start()

    def fwd_copy(o):
        d = peer(o)
        return send(amp.at[:, d], pairs.at[r, :, c], fwd_s.at[o], fwd_r.at[me], place(d))

    def lad_copy(o):
        return send(lad_own, lad_all.at[me], lad_s.at[o], lad_r.at[me], place(peer(o)))

    def fwd_start(lo, hi):
        @pl.loop(lo, hi)
        def _(o):
            fwd_copy(o).start()

    @pl.loop(1, nd)
    def _(n):
        lad_copy(n).start()

    fwd_start(1, nd)

    own_copies[1].wait()
    for k in range(occ_row):
        slab = amp_v[k].reshape(VIR, VIR).astype(F32)
        comb[k * VIR:(k + 1) * VIR, :] = (2.0 * slab - slab.T).astype(BF16)
    own_copies[2].wait()

    def tw_copy(q):
        return send(away.at[q], twin.at[q], tw_s.at[q], tw_r.at[q], (r, 2 * z + other))

    def s1_copy(q):
        return send(out1.at[q], in1.at[q], s1_s.at[q], s1_r.at[q], (r, 2 * near + core))

    def s2_copy(q):
        return send(out2.at[q], in2.at[q], s2_s.at[q], s2_r.at[q], (r, 2 * far + core))

    def g1_copy(q):
        return send(
            fit.at[z, core, q], fit.at[z, core, q], g1_s.at[q], g1_r.at[q], (r, 2 * far + core)
        )

    def g2_copy(which, q):
        src = far if which else z
        return send(
            fit.at[src, core, q], fit.at[src, core, q], g2_s.at[which, q], g2_r.at[which, q],
            (r, 2 * near + core),
        )

    def relay(src):
        return send(
            fit.at[src, core], fit.at[src, core], rl_s.at[src], rl_r.at[src], (r, 2 * z + other)
        )

    def partial_sums(q):
        got = jnp.dot(comb[...], factors[q], preferred_element_type=F32)
        got = got.reshape(Z, 2, chunk, q_cols)
        part[q] = got
        away[q] = part[q, :, other].astype(BF16)
        tw_copy(q).start()

    def pair_sum(q, to):
        return part[q, to, core] + twin[q, to].astype(F32)

    def near_sums(q):
        tw_copy(q).wait_recv()
        out1[q, 0] = pair_sum(q, near).astype(BF16)
        out1[q, 1] = pair_sum(q, far_near).astype(BF16)
        s1_copy(q).start()

    partial_sums(r)

    for copy in own_copies[4:]:
        copy.wait()
    ids_r = lax.broadcasted_iota(jnp.int32, (VIR, VIR), 0)
    ids_c = lax.broadcasted_iota(jnp.int32, (VIR, VIR), 1)
    e_col = jnp.sum(jnp.where(ids_r == ids_c, e_v[...], 0.0), axis=1, keepdims=True)
    v_row = jnp.sum(jnp.where(ids_r == m_v[...], e_col, 0.0), axis=0, keepdims=True)
    v_col = jnp.sum(jnp.where(ids_r == ids_c, v_row, 0.0), axis=1, keepdims=True)
    energy_j = occ_ev[occ_iv[c]]
    for k in range(occ_row):
        energy = occ_ev[occ_iv[r * occ_row + k]] + energy_j
        inverse[k * VIR:(k + 1) * VIR, :] = 1.0 / ((energy - v_col) - v_row)

    near_sums(r)

    @pl.loop(1, nd)
    def _(o):
        d = peer(o)
        send(lad_own, lad_all.at[d], lad_s.at[o], lad_r.at[d], place(d)).wait_recv()

    shift = sub.bit_length() - 1
    wide = n_pairs * sub
    lad_flat = lad_all[...].reshape(nd * lad_own.shape[0], lad_own.shape[1]).astype(BF16)
    spread = (
        lax.broadcasted_iota(jnp.int32, (lad_own.shape[1], wide), 0)
        == (lax.broadcasted_iota(jnp.int32, (lad_own.shape[1], wide), 1) >> shift)
    )
    lad_wide = jnp.dot(
        lad_flat, spread.astype(F32).astype(BF16), preferred_element_type=F32
    ).astype(BF16)
    step_rows = 128

    @pl.loop(0, wide // step_rows)
    def _(n):
        at = pl.multiple_of(n * step_rows, step_rows)
        pair = (lax.broadcasted_iota(jnp.int32, (step_rows, lad_flat.shape[0]), 0) + at) >> shift
        held = lax.broadcasted_iota(jnp.int32, (step_rows, lad_flat.shape[0]), 1)
        pick = held == (lax.div(pair, per_pair) * lad_own.shape[0] + lax.rem(pair, per_pair))
        block = jnp.dot(pick.astype(F32).astype(BF16), lad_wide, preferred_element_type=F32)
        same = (lax.broadcasted_iota(jnp.int32, (step_rows, wide), 0) & (sub - 1)) == (
            lax.broadcasted_iota(jnp.int32, (step_rows, wide), 1) & (sub - 1)
        )
        kron[pl.ds(at, step_rows), :] = jnp.where(same, block, 0.0).astype(BF16)

    for o in range(1, R):
        q = order[o]
        send(fac, factors.at[q], fac_s.at[o], fac_r.at[q], (r, c)).wait_recv()
        partial_sums(q)
        if o > 1:
            near_sums(order[o - 1])
    near_sums(order[R - 1])

    own_copies[3].wait()
    row_blocks = wide // R
    for o in range(R):
        source = lax.rem(r + R - o, R)

        @pl.loop(0 if o else 1, C)
        def _(n):
            dc = lax.rem(c + n, C)
            d = source * C + dc
            send(
                amp.at[:, d], pairs.at[source, :, dc], fwd_s.at[n], fwd_r.at[d], (source, dc)
            ).wait_recv()

        block = pairs[source].reshape(row_blocks, VIR)
        at = pl.multiple_of(source * row_blocks, row_blocks)
        for n in range(R):
            rows_n = slice(n * row_blocks, (n + 1) * row_blocks)
            term = jnp.dot(
                kron[rows_n, pl.ds(at, row_blocks)], block, preferred_element_type=F32
            )
            if o:
                term = held_sum[rows_n, :] + term
            if o < R - 1:
                held_sum[rows_n, :] = term
            else:
                hole[n] = term.astype(BF16).reshape(occ_row, C, sub, VIR)

    def back_copy(o):
        d = peer(o)
        dr, dc = place(d)
        return send(hole.at[dr, :, dc], hole_in.at[:, me], back_s.at[o], back_r.at[me], (dr, dc))

    @pl.loop(1, nd // 2)
    def _(o):
        back_copy(o).start()

    for q in order:
        s1_copy(q).wait_recv()
        out2[q] = (pair_sum(q, far) + in1[q, 1].astype(F32)).astype(BF16)
        s2_copy(q).start()

    @pl.loop(nd // 2, nd)
    def _(o):
        back_copy(o).start()

    hole_in[:, me] = hole[r, :, c]
    for q in range(R):
        turned[q] = factors[q].T


    for q in order:
        s2_copy(q).wait_recv()
        total = pair_sum(q, z) + in1[q, 0].astype(F32)
        fit[z, core, q] = (total + in2[q].astype(F32)).astype(BF16)
        g1_copy(q).start()
        g2_copy(0, q).start()
    relay(z).start()

    def g1_wait(q):
        send(
            fit.at[far, core, q], fit.at[far, core, q], g1_s.at[q], g1_r.at[q], (r, c)
        ).wait_recv()

    def g2_wait(which, q):
        src = far_near if which else near
        send(
            fit.at[src, core, q], fit.at[src, core, q], g2_s.at[which, q], g2_r.at[which, q],
            (r, c),
        ).wait_recv()

    per_occ = VIR // chunk
    groups = chunk // sub

    def rows_of(n):
        return pl.ds(pl.multiple_of(n * chunk, chunk), chunk)

    def fitted_dot(src, which):
        acc = None
        for q in range(R):
            term = jnp.dot(fit[src, which, q], turned[q], preferred_element_type=F32)
            acc = term if acc is None else acc + term
        return acc

    def finish(src, which, acc):
        n = 2 * src + which
        k = lax.div(n, per_occ)
        m = lax.rem(n, per_occ)
        held = hole_in[k, pl.ds(m * groups, groups)].reshape(chunk, VIR).astype(F32)
        out[rows_of(n), :] = ((acc + held) * inverse[rows_of(n), :]).astype(BF16)

    def relay_wait(src):
        send(
            fit.at[src, other], fit.at[src, other], rl_s.at[src], rl_r.at[src], (r, c)
        ).wait_recv()

    coul[0] = fitted_dot(z, core)
    for q in order:
        g1_wait(q)
        g2_copy(1, q).start()
    relay(far).start()
    coul[1] = fitted_dot(far, core)
    relay_wait(z)
    coul[2] = fitted_dot(z, other)
    relay_wait(far)
    coul[3] = fitted_dot(far, other)

    @pl.loop(1, nd)
    def _(o):
        d = peer(o)
        send(hole.at[r, :, c], hole_in.at[:, d], back_s.at[o], back_r.at[d], place(d)).wait_recv()

    finish(z, core, coul[0])
    finish(far, core, coul[1])
    finish(z, other, coul[2])
    finish(far, other, coul[3])
    for which, src in ((0, near), (1, far_near)):
        for q in order:
            g2_wait(which, q)
        relay(src).start()
        finish(src, core, fitted_dot(src, core))
    for src in (near, far_near):
        relay_wait(src)
        finish(src, other, fitted_dot(src, other))

    @pl.loop(1, nd)
    def _(o):
        fwd_copy(o).wait_send()
        lad_copy(o).wait_send()
        back_copy(o).wait_send()

    for o in range(1, R):
        fac_copy(o).wait_send()
    for q in range(R):
        tw_copy(q).wait_send()
        s1_copy(q).wait_send()
        s2_copy(q).wait_send()
        g1_copy(q).wait_send()
        g2_copy(0, q).wait_send()
        g2_copy(1, q).wait_send()
    for o in range(Z):
        relay(o).wait_send()


def fused(R, C, amplitudes, df_factors, ladder, occ_energy, occ_index, vir_energy, vir_map):
    nd = R * C
    Z = C // 2
    rows, _ = amplitudes.shape
    occ_row = rows // VIR
    sub = VIR // nd
    chunk = rows // C
    depth, q_cols = df_factors.shape
    n_pairs = ladder.shape[1]
    wide = n_pairs * sub
    lad_rows = -(-ladder.shape[0] // 8) * 8
    lad_cols = -(-n_pairs // 128) * 128
    hbm = pl.BlockSpec(memory_space=pl.ANY)
    dma = pltpu.SemaphoreType.DMA
    return pl.pallas_call(
        functools.partial(kernel, R, C),
        out_shape=jax.ShapeDtypeStruct((rows, VIR), BF16),
        in_specs=[hbm] * 7,
        out_specs=pl.BlockSpec(memory_space=pltpu.VMEM),
        scratch_shapes=[
            pltpu.VMEM((occ_row, nd, sub, VIR), BF16),
            pltpu.VMEM(ladder.shape, BF16),
            pltpu.VMEM((1, VIR), F32),
            pltpu.VMEM((1, VIR), jnp.int32),
            pltpu.SMEM(occ_energy.shape, F32),
            pltpu.SMEM(occ_index.shape, jnp.int32),
            pltpu.VMEM((rows, VIR), BF16),
            pltpu.VMEM((R, depth, q_cols), BF16),
            pltpu.VMEM((R, q_cols, depth), BF16),
            pltpu.VMEM((R, Z, 2, chunk, q_cols), F32),
            pltpu.VMEM((R, Z, chunk, q_cols), BF16),
            pltpu.VMEM((R, Z, chunk, q_cols), BF16),
            pltpu.VMEM((R, 2, chunk, q_cols), BF16),
            pltpu.VMEM((R, 2, chunk, q_cols), BF16),
            pltpu.VMEM((R, chunk, q_cols), BF16),
            pltpu.VMEM((R, chunk, q_cols), BF16),
            pltpu.VMEM((Z, 2, R, chunk, q_cols), BF16),
            pltpu.VMEM((R, occ_row, C, sub, VIR), BF16),
            pltpu.VMEM((R, occ_row, C, sub, VIR), BF16),
            pltpu.VMEM((occ_row, nd, sub, VIR), BF16),
            pltpu.VMEM((wide, wide), BF16),
            pltpu.VMEM((lad_rows, lad_cols), F32),
            pltpu.VMEM((nd, lad_rows, lad_cols), F32),
            pltpu.VMEM((rows, VIR), F32),
            pltpu.VMEM((4, chunk, VIR), F32),
            pltpu.VMEM((wide, VIR), F32),
            dma((8,)),
            dma((R,)), dma((R,)),
            dma((nd,)), dma((nd,)),
            dma((nd,)), dma((nd,)),
            dma((R,)), dma((R,)),
            dma((R,)), dma((R,)),
            dma((R,)), dma((R,)),
            dma((R,)), dma((R,)),
            dma((2, R)), dma((2, R)),
            dma((Z,)), dma((Z,)),
            dma((nd,)), dma((nd,)),
        ],
        compiler_params=pltpu.CompilerParams(
            collective_id=0, has_side_effects=True, vmem_limit_bytes=56 * 2**20
        ),
    )(
        amplitudes.reshape(occ_row, nd, sub, VIR), df_factors, ladder, occ_energy, occ_index,
        vir_energy.reshape(1, VIR), vir_map.reshape(1, VIR),
    )


def shards(amplitudes, df_factors, *rest):
    R, C = lax.axis_size("row"), lax.axis_size("col")
    rows, cols = amplitudes.shape
    fits = (
        VIR % (16 * R * C) == 0
        and cols == VIR
        and (R, C) == (4, 8)
        and rows % (16 * C) == 0
        and VIR % (rows // C) == 0
        and (rows // C) % (VIR // (R * C)) == 0
        and df_factors.shape[1] % 128 == 0
    )
    if fits:
        return fused(R, C, amplitudes, df_factors, *rest)
    return by_collectives(amplitudes, df_factors, *rest)


def solution(mesh):
    placed = (P("row", "col"), P("col", "row"), P(("row", "col"), None), P(), P(), P(), P())
    return jax.shard_map(
        shards, mesh=mesh, in_specs=placed, out_specs=P("row", "col"), check_vma=False
    )
```
